32 devices in a mesh: dp: 8 (over y, x, core), pipe: 4 (over z).
Axes of the slice: x: 2, y: 2, z: 4, core: 2. Of those that a mesh axis runs over, the one named last changes fastest.
Arguments:
- master: float32 [4, 128, 8192], P('pipe', 'dp'), may hold values from -0.12 to 0.12
- moment1: float32 [4, 128, 8192], P('pipe', 'dp'), may hold values from -3 to 3
- moment2: float32 [4, 128, 8192], P('pipe', 'dp'), may hold values from 0.25 to 4.5
- quant_grad: bfloat16 [4, 128, 8192], P('pipe', 'dp'), may hold values from -120 to 120
- grad_exponent: int32 [4, 128], P('pipe', 'dp'), may hold values from -3 to 2
- replica_params: bfloat16 [4, 8, 128, 8192], P('pipe', 'dp'), as said below
- failed: int32 [4, 2], replicated, may hold values from 0 to 7, as said below
- dest: int32 [4, 128], replicated, may hold values from 0 to 127, as said below
Outputs:
- new_master: float32 [4, 128, 8192], P('pipe', 'dp')
- new_moment1: float32 [4, 128, 8192], P('pipe', 'dp')
- new_moment2: float32 [4, 128, 8192], P('pipe', 'dp')
The draws below stay inside these ranges and needn't reach their ends.
Inputs may be any that keep to these rules, and one draw needn't show every extreme that they name: `failed`: each group lists 2 distinct ranks; group 0 lists ranks 1 and 4; in every other group some rows of the first listed rank have new positions among the rows of the second listed rank (new position // 16). `dest`: each group's row is a permutation of its rows; the 16 rows of one rank (old rows r * 16 to r * 16 + 15) land in at most 2 rows of any one rank's new rows (new position // 16), and some pair of ranks reaches 2 in every group. `replica_params`: within a group the copies of ranks not listed in failed are equal; the copies of listed ranks are zero.
All inputs are finite; a program needn't handle non-finite values.
Results may differ from the reference program's by a relative error of at most 0.0003.
Values may be sent and summed in bfloat16 or wider, within the bound.
No kernel may reach another device: no remote copies, remote signals or barrier semaphores. Data moves between devices by JAX's collectives and lax.ppermute only.
A program may use at most 64 MiB of HBM per device.

```python
import math
import jax
import jax.numpy as jnp
from jax import lax

D = 8192
K = 16
FMAX = 2
STEP = 20
RANKS = 8
GROUPS = 4
GROUP_ROWS = 128
CAP = 2


def group_dest(group_key):
    per_layer = K // CAP
    first_key = jax.random.fold_in(group_key, 1)
    base_perm = jax.random.permutation(first_key, RANKS)
    layer_perms = []
    layer_offsets = []
    for layer in range(CAP):
        rest_perm = 1 + jax.random.permutation(jax.random.fold_in(group_key, 100 + layer), RANKS - 1)
        mixer = jnp.concatenate([jnp.zeros((1,), jnp.int32), rest_perm.astype(jnp.int32)])
        layer_perms.append(base_perm[mixer])
        offset_pick = 1 + jax.random.permutation(jax.random.fold_in(group_key, 200 + layer), RANKS - 1)
        layer_offsets.append(jnp.concatenate([jnp.zeros((1,), jnp.int32), offset_pick[:per_layer - 1].astype(jnp.int32)]))
    taus = jnp.stack(layer_perms)
    offsets = jnp.stack(layer_offsets)
    targets = ((taus.T[:, :, None] + offsets[None, :, :]) % RANKS).reshape(RANKS, K)
    row_keys = jax.random.split(jax.random.fold_in(group_key, 3), RANKS)
    row_perm = jax.vmap(lambda row_key: jax.random.permutation(row_key, K))(row_keys)
    target_rows = jnp.take_along_axis(targets, row_perm, axis=1).reshape(-1)
    scores = jax.random.permutation(jax.random.fold_in(group_key, 4), GROUP_ROWS)
    same_target = target_rows[None, :] == target_rows[:, None]
    before = scores[None, :] < scores[:, None]
    slot_index = jnp.sum((same_target & before).astype(jnp.int32), axis=1)
    return (target_rows * K + slot_index).astype(jnp.int32)


def group_failed(group_key, dest_row, group_index):
    order_scores = jax.random.permutation(jax.random.fold_in(group_key, 5), RANKS).astype(jnp.int32)
    pick_scores = jax.random.permutation(jax.random.fold_in(group_key, 6), RANKS).astype(jnp.int32)
    first_rank = jnp.argmax(order_scores).astype(jnp.int32)
    old_rank = (jnp.arange(GROUP_ROWS, dtype=jnp.int32) // K).astype(jnp.int32)
    new_rank = (dest_row // K).astype(jnp.int32)
    from_first = old_rank == first_rank
    rank_ids = jnp.arange(RANKS, dtype=jnp.int32)
    reach = jnp.any(from_first[None, :] & (new_rank[None, :] == rank_ids[:, None]), axis=1)
    ranking = jnp.where(rank_ids == first_rank, 3 * RANKS, jnp.where(reach, 2 * RANKS + pick_scores, pick_scores))
    drawn = lax.top_k(ranking.astype(jnp.int32), FMAX)[1].astype(jnp.int32)
    fixed = jnp.array([1, RANKS // 2], dtype=jnp.int32)
    return jnp.where(group_index == 0, fixed, drawn).astype(jnp.int32)


def group_keys_of(key):
    return jax.random.split(jax.random.fold_in(key, 21), GROUPS)


def draw_dest(key, part):
    return jax.vmap(group_dest)(group_keys_of(key))


def failed_ranks(key):
    group_keys = group_keys_of(key)
    dests = jax.vmap(group_dest)(group_keys)
    return jax.vmap(group_failed)(group_keys, dests, jnp.arange(GROUPS, dtype=jnp.int32)).astype(jnp.int32)


def draw_failed(key, part):
    return failed_ranks(key)


def draw_replica_params(key, part):
    lost_ranks = failed_ranks(key)
    base_rows = jax.random.normal(jax.random.fold_in(key, 12), (GROUPS, GROUP_ROWS, D), jnp.float32) * 0.02
    rank_ids = jnp.arange(RANKS, dtype=jnp.int32)
    is_failed = jnp.any(rank_ids[None, :, None] == lost_ranks[:, None, :], axis=2)
    return jnp.where(is_failed[:, :, None, None], jnp.float32(0.0), base_rows[:, None, :, :]).astype(jnp.bfloat16)


def draw_grad_exponent(key, part):
    base_exp = jax.random.randint(jax.random.fold_in(key, 30), (GROUPS, GROUP_ROWS), -3, 2)
    trend = 2 * (jnp.arange(GROUP_ROWS) // K) // RANKS
    return (base_exp + trend[None, :]).astype(jnp.int32)


def draw_quant_grad(key, part):
    noise = jnp.clip(jax.random.normal(jax.random.fold_in(key, 41), (GROUPS, GROUP_ROWS, D), jnp.float32), -5.0, 5.0)
    column_draw = jax.random.uniform(jax.random.fold_in(key, 42), (D,), jnp.float32)
    column_scale = jnp.exp(column_draw * math.log(10.0))
    return (noise * column_scale[None, None, :]).astype(jnp.bfloat16)


def draw_master(key, part):
    sub_key = jax.random.fold_in(key, 51)
    noise = jax.random.normal(jax.random.fold_in(sub_key, 3), (GROUPS, GROUP_ROWS, D), jnp.float32)
    return jnp.clip(noise, -6.0, 6.0) * 0.02


def draw_moment1(key, part):
    sub_key = jax.random.fold_in(key, 61)
    noise = jax.random.normal(jax.random.fold_in(sub_key, 3), (GROUPS, GROUP_ROWS, D), jnp.float32)
    return jnp.clip(noise, -6.0, 6.0) * 0.5


def draw_moment2(key, part):
    level_draw = jax.random.uniform(jax.random.fold_in(key, 71), (GROUPS, GROUP_ROWS, D), jnp.float32)
    return jnp.exp(math.log(0.25) + level_draw * math.log(16.0))


def setup_inputs(seed: int = 0) -> dict:
    keys = jax.random.split(jax.random.key(seed), 9)
    return {
        "master": draw_master(jax.random.fold_in(keys[8], 71), 0),
        "moment1": draw_moment1(jax.random.fold_in(keys[8], 71), 0),
        "moment2": draw_moment2(jax.random.fold_in(keys[8], 71), 0),
        "quant_grad": draw_quant_grad(jax.random.fold_in(keys[8], 71), 0),
        "grad_exponent": draw_grad_exponent(jax.random.fold_in(keys[8], 71), 0),
        "replica_params": draw_replica_params(jax.random.fold_in(keys[8], 71), 0),
        "failed": draw_failed(jax.random.fold_in(keys[8], 71), 0),
        "dest": draw_dest(jax.random.fold_in(keys[8], 71), 0),
    }


beta_one = 0.9
beta_two = 0.95
learn_rate = 0.00015
decay_rate = 0.1
adam_eps = 1e-08
clip_eps = 1e-06

def adam_step(weights, first, second, grads):
    first_new = beta_one * first + (1.0 - beta_one) * grads
    second_new = beta_two * second + (1.0 - beta_two) * grads * grads
    corr_one = 1.0 - beta_one ** STEP
    corr_two = 1.0 - beta_two ** STEP
    direction = first_new / corr_one / (jnp.sqrt(second_new / corr_two) + adam_eps) + decay_rate * weights
    return (weights - learn_rate * direction, first_new, second_new)

def reference(master, moment1, moment2, quant_grad, grad_exponent, replica_params, failed, dest):
    grad = quant_grad.astype(jnp.float32) * jnp.exp2(grad_exponent.astype(jnp.float32))[:, :, None]
    grad_total = jnp.sum(grad * grad)
    clip_scale = jnp.minimum(1.0, 1.0 / jnp.sqrt(grad_total / (GROUPS * GROUP_ROWS * D) + clip_eps))
    clipped = grad * clip_scale
    rank_ids = jnp.arange(RANKS, dtype=jnp.int32)
    is_alive = jnp.all(rank_ids[None, :, None] != failed[:, None, :], axis=2)
    root_rank = lax.optimization_barrier(jnp.min(jnp.where(is_alive, rank_ids[None, :], RANKS), axis=1)).astype(jnp.int32)
    copy_rows = replica_params[jnp.arange(GROUPS, dtype=jnp.int32), root_rank].astype(jnp.float32)
    row_rank = (jnp.arange(GROUP_ROWS, dtype=jnp.int32) // K).astype(jnp.int32)
    is_lost = jnp.any(row_rank[None, :, None] == failed[:, None, :], axis=2)[:, :, None]
    start_master = jnp.where(is_lost, copy_rows, master)
    start_first = jnp.where(is_lost, jnp.float32(0.0), moment1)
    start_second = jnp.where(is_lost, jnp.float32(0.0), moment2)
    w_next, m_next, v_next = adam_step(start_master, start_first, start_second, clipped)
    group_ids = jnp.broadcast_to(jnp.arange(GROUPS, dtype=jnp.int32)[:, None], dest.shape)
    out_master = jnp.zeros_like(w_next).at[group_ids, dest].set(w_next)
    out_first = jnp.zeros_like(m_next).at[group_ids, dest].set(m_next)
    out_second = jnp.zeros_like(v_next).at[group_ids, dest].set(v_next)
    return (out_master, out_first, out_second)
```

```python
import functools

import jax
import jax.numpy as jnp
import numpy as np
from jax import lax
from jax.experimental import pallas as pl
from jax.experimental.pallas import tpu as pltpu
from jax.sharding import PartitionSpec as P

STEP = 20

beta_one = 0.9
beta_two = 0.95
learn_rate = 0.00015
decay_rate = 0.1
adam_eps = 1e-08
clip_eps = 1e-06

MASTER_MAX = 0.12
FIRST_MAX = 3.0
SECOND_MIN = 0.25
SECOND_MAX = 4.5

OCTAVES = 12
LOG_TOP = float(np.log(1.0 + 2.0**OCTAVES))
LOG_STEPS = 32767.0
SECOND_STEPS = 65535.0

COLUMN_CHUNKS = 4
VMEM_LIMIT = 56 * 1024 * 1024
ANY = pl.BlockSpec(memory_space=pl.ANY)


def encode_log(x, top):
    steps = jnp.log(1.0 + jnp.abs(x) * (2.0**OCTAVES / top)) * (LOG_STEPS / LOG_TOP) + 0.5
    code = jnp.minimum(steps, LOG_STEPS).astype(jnp.int32)
    return jnp.where(x < 0, -code, code)


def decode_log(code, top):
    size = (jnp.exp(jnp.abs(code).astype(jnp.float32) * (LOG_TOP / LOG_STEPS)) - 1.0) * (top / 2.0**OCTAVES)
    return jnp.where(code < 0, -size, size)


def encode_second(x):
    steps = (x - SECOND_MIN) * (SECOND_STEPS / (SECOND_MAX - SECOND_MIN)) + 0.5
    return jnp.clip(steps, 0.0, SECOND_STEPS).astype(jnp.int32)


def decode_second(code):
    return code.astype(jnp.float32) * ((SECOND_MAX - SECOND_MIN) / SECOND_STEPS) + SECOND_MIN


def encode_short(x):
    size = jnp.abs(x)
    is_zero = size < 2.0**-126
    size = jnp.where(is_zero, 1.0, size)
    exponent = jnp.floor(jnp.log2(size) + 0.002)
    half = jnp.floor(exponent * 0.5)
    mantissa = size * jnp.exp2(-half) * jnp.exp2(half - exponent) * 128.0
    code = exponent * 128.0 + (127.0 * 128.0 - 128.0) + mantissa
    code = jnp.where(is_zero, 0.0, code + 0.5).astype(jnp.int32)
    return jnp.where(x < 0, -code, code)


def decode_short(code):
    size = jnp.abs(code)
    exponent = lax.shift_right_logical(size, 7)
    mantissa = (size & 127).astype(jnp.float32) * (1.0 / 128.0) + 1.0
    scale = jnp.where(exponent > 0, jnp.exp2((exponent - 127).astype(jnp.float32)), 0.0)
    value = mantissa * scale
    return jnp.where(code < 0, -value, value)


def join(high, low):
    return (high << 16) | (low & 0xFFFF)


def signed_high(word):
    return word >> 16


def signed_low(word):
    return (word << 16) >> 16


def extra_columns(k, width):
    return {1: width // 2, 2: width // 4, 4: width // 4}.get(k, 0)


def pack_kernel(
    ranks, cap, fails, devices,
    dest, failed, grad_exponent, master, moment1, moment2, quant_grad, replica,
    *refs,
):
    payloads, total = refs[:ranks], refs[ranks]
    (dest_s, failed_s, exponent_s, counts, table, lost_counts, lost_table,
     master_v, first_v, second_v, grad_v, block_v, lost_v, picked_v, word_one, word_two, extra_v,
     small_sem, in_sem, block_sem, pick_sem, out_sem) = refs[ranks + 1:]
    rows, width = master_v.shape
    half, quarter = width // 2, width // 4
    chunk = width // COLUMN_CHUNKS
    group = lax.axis_index("pipe")
    me = lax.axis_index("dp")

    small = [
        pltpu.make_async_copy(failed, failed_s, small_sem.at[0]),
        pltpu.make_async_copy(grad_exponent, exponent_s, small_sem.at[1]),
        pltpu.make_async_copy(dest, dest_s, small_sem.at[2]),
    ]
    for copy in small:
        copy.start()
    loads = []
    for part in range(COLUMN_CHUNKS):
        columns = pl.ds(part * chunk, chunk)
        copies = [
            pltpu.make_async_copy(source.at[:, columns], target.at[:, columns], in_sem.at[part, i])
            for i, (source, target) in enumerate(
                [(quant_grad, grad_v), (master, master_v), (moment1, first_v), (moment2, second_v)]
            )
        ]
        for copy in copies:
            copy.start()
        loads.append(copies)
    for copy in small:
        copy.wait()
    blocks = [
        pltpu.make_async_copy(
            replica.at[pl.ds(pl.multiple_of(failed_s[group, i] * rows, rows), rows), :],
            block_v.at[pl.ds(i * rows, rows), :],
            block_sem.at[i],
        )
        for i in range(fails)
    ]
    for copy in blocks:
        copy.start()

    for i in range(ranks * cap):
        table[i] = 0
    for i in range(ranks):
        counts[i] = 0
    for r in range(rows):
        target = lax.div(dest_s[group, me * rows + r], rows)
        order = counts[target]
        table[target * cap + order] = r
        counts[target] = order + 1
    for i in range(ranks * fails * cap):
        lost_table[i] = 0
    for i in range(ranks * fails):
        lost_counts[i] = 0
    for i in range(fails):
        for r in range(rows):
            target = lax.div(dest_s[group, failed_s[group, i] * rows + r], rows)
            slot = target * fails + i
            order = lost_counts[slot]
            lost_table[slot * cap + order] = i * rows + r
            lost_counts[slot] = order + 1

    row_ids = lax.broadcasted_iota(jnp.int32, (rows, 128), 0)
    exponents = jnp.zeros((rows, 128), jnp.float32)
    for r in range(rows):
        exponents = jnp.where(row_ids == r, exponent_s[0, r].astype(jnp.float32), exponents)
    row_scale = jnp.exp2(exponents)[:, :1]

    for copy in blocks:
        copy.wait()
    for part in range(COLUMN_CHUNKS):
        columns = pl.ds(part * chunk, chunk)
        lost_v[:, columns] = block_v[:, columns].astype(jnp.float32)
    lost_rows = fails * cap
    picks = []
    for j in range(lost_rows):
        one = lost_table[(me ^ 1) * lost_rows + j]
        two = lost_table[(me ^ 2) * lost_rows + j]
        four = lost_table[(me ^ 4) * lost_rows + j]
        picks.append((lost_v.at[pl.ds(one, 1), :], picked_v.at[pl.ds(j, 1), :]))
        for q, source in ((0, two), (2, two), (1, four), (3, four)):
            columns = pl.ds(q * quarter, quarter)
            picks.append((lost_v.at[pl.ds(source, 1), columns], picked_v.at[pl.ds(lost_rows + j, 1), columns]))
    picks = [pltpu.make_async_copy(a, b, pick_sem) for a, b in picks]
    for copy in picks:
        copy.start()

    sums = jnp.zeros((8, 128), jnp.float32)
    outs = []
    for part in range(COLUMN_CHUNKS):
        columns = pl.ds(part * chunk, chunk)
        for copy in loads[part]:
            copy.wait()
        grad = grad_v[:, columns].astype(jnp.float32) * row_scale
        sums += jnp.sum((grad * grad).reshape(rows // 8, 8, chunk // 128, 128), axis=(0, 2))
        word_one[:, columns] = join(encode_log(master_v[:, columns], MASTER_MAX), encode_log(first_v[:, columns], FIRST_MAX))
        word_two[:, columns] = join(encode_second(second_v[:, columns]), encode_short(grad))
        for k in reversed(range(ranks)):
            for order in range(cap):
                row = table[(me ^ k) * cap + order]
                for i, word in enumerate((word_one, word_two)):
                    copy = pltpu.make_async_copy(
                        word.at[pl.ds(row, 1), columns],
                        payloads[k].at[pl.ds(i * cap + order, 1), columns],
                        out_sem,
                    )
                    copy.start()
                    outs.append(copy)
    total[...] = jnp.broadcast_to(jnp.sum(sums, axis=0, keepdims=True), (devices, 128))

    for copy in picks:
        copy.wait()
    extra_v[...] = join(encode_short(picked_v[:, :half]), encode_short(picked_v[:, half:]))
    for k, first_row, first_column in ((1, 0, 0), (2, lost_rows, 0), (4, lost_rows, quarter)):
        columns = extra_columns(k, width)
        copy = pltpu.make_async_copy(
            extra_v.at[pl.ds(first_row, lost_rows), pl.ds(first_column, columns)],
            payloads[k].at[:, pl.ds(width, columns)],
            out_sem,
        )
        copy.start()
        outs.append(copy)
    for copy in outs:
        copy.wait()


def base_kernel(
    ranks, cap, fails,
    dest, failed, replica, from_one, from_two, from_four,
    base, lost, places,
    dest_s, failed_s, counts, places_s, lost_counts, lost_places, lost_sources,
    block_v, rows_v, extra_v, small_sem, block_sem, move_sem,
):
    rows, width = lost.shape[0], base.shape[1]
    half, quarter = width // 2, width // 4
    lost_rows = fails * cap
    group = lax.axis_index("pipe")
    me = lax.axis_index("dp")
    small = [
        pltpu.make_async_copy(failed, failed_s, small_sem.at[0]),
        pltpu.make_async_copy(dest, dest_s, small_sem.at[1]),
    ]
    for copy in small:
        copy.start()
    for copy in small:
        copy.wait()
    blocks = [
        pltpu.make_async_copy(
            replica.at[pl.ds(pl.multiple_of(failed_s[group, i] * rows, rows), rows), :],
            block_v.at[pl.ds(i * rows, rows), :],
            block_sem.at[i],
        )
        for i in range(fails)
    ]
    for copy in blocks:
        copy.start()

    for i in range(ranks * cap):
        places_s[0, i] = -1
    for i in range(ranks):
        counts[i] = 0

    @pl.loop(0, ranks * rows)
    def _(row):
        place = dest_s[group, row]

        @pl.when(lax.div(place, rows) == me)
        def _():
            source = lax.div(row, rows)
            order = counts[source]
            places_s[0, source * cap + order] = lax.rem(place, rows)
            counts[source] = order + 1

    row_ids = lax.broadcasted_iota(jnp.int32, (rows, 128), 0)
    mask = jnp.zeros((rows, 128), jnp.float32)
    for i in range(fails):
        lost_counts[i] = 0
        for order in range(cap):
            place = places_s[0, failed_s[group, i] * cap + order]
            lost_places[i * cap + order] = place
            lost_sources[i * cap + order] = 0
            mask = jnp.where(row_ids == place, 1.0, mask)
        for r in range(rows):

            @pl.when(lax.div(dest_s[group, failed_s[group, i] * rows + r], rows) == me)
            def _(i=i, r=r):
                order = lost_counts[i]
                lost_sources[i * cap + order] = i * rows + r
                lost_counts[i] = order + 1

    lost[...] = mask
    send_places = pltpu.make_async_copy(places_s, places, small_sem.at[0])
    send_places.start()

    for copy in blocks:
        copy.wait()
    is_failed = failed_s[group, 0] == me
    sibling_failed = failed_s[group, 0] == (me ^ 1)
    for i in range(1, fails):
        is_failed = is_failed | (failed_s[group, i] == me)
        sibling_failed = sibling_failed | (failed_s[group, i] == (me ^ 1))

    @pl.when(jnp.logical_not(is_failed))
    def _():
        rows_v[...] = block_v[...].astype(jnp.float32)

    @pl.when(is_failed)
    def _():
        @pl.when(jnp.logical_not(sibling_failed))
        def _():
            copy = pltpu.make_async_copy(from_one.at[:, pl.ds(width, half)], extra_v, move_sem)
            copy.start()
            copy.wait()

        @pl.when(sibling_failed)
        def _():
            copies = [
                pltpu.make_async_copy(
                    ref.at[:, pl.ds(width, quarter)], extra_v.at[:, pl.ds(i * quarter, quarter)], move_sem
                )
                for i, ref in enumerate((from_two, from_four))
            ]
            for copy in copies:
                copy.start()
            for copy in copies:
                copy.wait()

        words = extra_v[...]
        rows_v[0:lost_rows, 0:half] = decode_short(signed_high(words))
        rows_v[0:lost_rows, half:width] = decode_short(signed_low(words))
        for j in range(lost_rows):
            lost_sources[j] = j

    def move(j):
        return pltpu.make_async_copy(
            rows_v.at[pl.ds(lost_sources[j], 1), :], base.at[pl.ds(lost_places[j], 1), :], move_sem
        )

    for j in range(lost_rows):

        @pl.when(lost_places[j] >= 0)
        def _(j=j):
            move(j).start()

    for j in range(lost_rows):

        @pl.when(lost_places[j] >= 0)
        def _(j=j):
            move(j).wait()

    send_places.wait()


def update_kernel(
    ranks, cap, elements,
    sums, lost, base, places, *refs,
):
    arrived = refs[:ranks]
    (new_master, new_first, new_second, places_s, word_one, word_two, base_v,
     master_o, first_o, second_o, small_sem, move_sem, base_sem, out_sem) = refs[ranks:]
    rows, width = word_one.shape
    chunk = width // COLUMN_CHUNKS
    me = lax.axis_index("dp")
    load_places = pltpu.make_async_copy(places, places_s, small_sem)
    load_places.start()
    load_base = pltpu.make_async_copy(base, base_v, base_sem)
    load_base.start()
    load_places.wait()

    def moves(k, order, part):
        place = places_s[0, (me ^ k) * cap + order]
        columns = pl.ds(part * chunk, chunk)
        return [
            pltpu.make_async_copy(
                arrived[k].at[pl.ds(i * cap + order, 1), columns],
                word.at[pl.ds(jnp.maximum(place, 0), 1), columns],
                move_sem.at[part],
            )
            for i, word in enumerate((word_one, word_two))
        ], place

    full = ranks * cap == rows
    for part in range(COLUMN_CHUNKS):
        for k in range(ranks):
            for order in range(cap):
                copies, place = moves(k, order, part)
                if full:
                    for copy in copies:
                        copy.start()
                else:

                    @pl.when(place >= 0)
                    def _(copies=copies):
                        for copy in copies:
                            copy.start()

    grad_total = jnp.sum(jnp.sum(sums[...], axis=0, keepdims=True), axis=1, keepdims=True)
    clip_scale = jnp.minimum(1.0, 1.0 / jnp.sqrt(grad_total / elements + clip_eps))
    is_lost = lost[:, :1] > 0.5
    load_base.wait()
    outs = []
    for part in range(COLUMN_CHUNKS):
        columns = pl.ds(part * chunk, chunk)
        for word in (word_one, word_two):
            pltpu.make_async_copy(word.at[:, columns], word.at[:, columns], move_sem.at[part]).wait()
        one, two = word_one[:, columns], word_two[:, columns]
        weights = jnp.where(is_lost, base_v[:, columns], decode_log(signed_high(one), MASTER_MAX))
        first = jnp.where(is_lost, 0.0, decode_log(signed_low(one), FIRST_MAX))
        second = jnp.where(is_lost, 0.0, decode_second(lax.shift_right_logical(two, 16)))
        grads = decode_short(signed_low(two)) * clip_scale
        first_new = beta_one * first + (1.0 - beta_one) * grads
        second_new = beta_two * second + (1.0 - beta_two) * grads * grads
        corr_one = 1.0 - beta_one**STEP
        corr_two = 1.0 - beta_two**STEP
        direction = first_new / corr_one / (jnp.sqrt(second_new / corr_two) + adam_eps) + decay_rate * weights
        master_o[:, columns] = weights - learn_rate * direction
        first_o[:, columns] = first_new
        second_o[:, columns] = second_new
        for source, target in ((master_o, new_master), (first_o, new_first), (second_o, new_second)):
            copy = pltpu.make_async_copy(source.at[:, columns], target.at[:, columns], out_sem)
            copy.start()
            outs.append(copy)
    for copy in outs:
        copy.wait()


def local(master, moment1, moment2, quant_grad, grad_exponent, replica_params, failed, dest):
    ranks = lax.axis_size("dp")
    devices = ranks * lax.axis_size("pipe")
    _, rows, width = master.shape
    fails = failed.shape[1]
    cap = (rows + ranks - 1) // ranks
    lost_rows = fails * cap
    params = pltpu.CompilerParams(vmem_limit_bytes=VMEM_LIMIT)
    i32, f32 = jnp.int32, jnp.float32
    vmem, smem, dma = pltpu.VMEM, pltpu.SMEM, pltpu.SemaphoreType.DMA

    packed = pl.pallas_call(
        functools.partial(pack_kernel, ranks, cap, fails, devices),
        out_shape=[jax.ShapeDtypeStruct((2 * cap, width + extra_columns(k, width)), i32) for k in range(ranks)]
        + [jax.ShapeDtypeStruct((devices, 128), f32)],
        in_specs=[ANY] * 8,
        out_specs=[ANY] * ranks + [pl.BlockSpec(memory_space=pltpu.VMEM)],
        scratch_shapes=[
            smem(dest.shape, i32), smem(failed.shape, i32), smem((1, rows), i32),
            smem((ranks,), i32), smem((ranks * cap,), i32),
            smem((ranks * fails,), i32), smem((ranks * lost_rows,), i32),
            vmem((rows, width), f32), vmem((rows, width), f32), vmem((rows, width), f32),
            vmem((rows, width), jnp.bfloat16),
            vmem((fails * rows, width), jnp.bfloat16), vmem((fails * rows, width), f32),
            vmem((2 * lost_rows, width), f32),
            vmem((rows, width), i32), vmem((rows, width), i32),
            vmem((2 * lost_rows, width // 2), i32),
            dma((3,)), dma((COLUMN_CHUNKS, 4)), dma((fails,)), dma, dma,
        ],
        compiler_params=params,
        name="pack",
    )(dest, failed, grad_exponent, master[0], moment1[0], moment2[0], quant_grad[0], replica_params[0, 0])
    payloads, total = packed[:ranks], packed[ranks]

    arrived = {0: payloads[0]}
    for k in [k for k in (1, 4, 2) if k < ranks] + [k for k in reversed(range(ranks)) if k not in (0, 1, 2, 4)]:
        arrived[k] = lax.ppermute(payloads[k], "dp", [(i, i ^ k) for i in range(ranks)])
    sums = lax.all_to_all(total, ("pipe", "dp"), split_axis=0, concat_axis=0, tiled=True)

    base, lost, places = pl.pallas_call(
        functools.partial(base_kernel, ranks, cap, fails),
        out_shape=[
            jax.ShapeDtypeStruct((rows, width), f32),
            jax.ShapeDtypeStruct((rows, 128), f32),
            jax.ShapeDtypeStruct((1, ranks * cap), i32),
        ],
        in_specs=[ANY] * 6,
        out_specs=[ANY, pl.BlockSpec(memory_space=pltpu.VMEM), ANY],
        scratch_shapes=[
            smem(dest.shape, i32), smem(failed.shape, i32), smem((ranks,), i32), smem((1, ranks * cap), i32),
            smem((fails,), i32), smem((lost_rows,), i32), smem((lost_rows,), i32),
            vmem((fails * rows, width), jnp.bfloat16), vmem((fails * rows, width), f32),
            vmem((lost_rows, width // 2), i32),
            dma((2,)), dma((fails,)), dma,
        ],
        compiler_params=params,
        name="base",
    )(dest, failed, replica_params[0, 0], arrived[1], arrived[2], arrived[4])

    outs = pl.pallas_call(
        functools.partial(update_kernel, ranks, cap, devices * rows * width),
        out_shape=[jax.ShapeDtypeStruct((rows, width), f32)] * 3,
        in_specs=[pl.BlockSpec(memory_space=pltpu.VMEM)] * 2 + [ANY] * (2 + ranks),
        out_specs=[ANY] * 3,
        scratch_shapes=[
            smem((1, ranks * cap), i32),
            vmem((rows, width), i32), vmem((rows, width), i32), vmem((rows, width), f32),
            vmem((rows, width), f32), vmem((rows, width), f32), vmem((rows, width), f32),
            dma, dma((COLUMN_CHUNKS,)), dma, dma,
        ],
        compiler_params=params,
        name="update",
    )(sums, lost, base, places, *[arrived[k] for k in range(ranks)])
    return tuple(out[None] for out in outs)


def solution(mesh):
    rows3 = P("pipe", "dp", None)
    in_specs = (rows3, rows3, rows3, rows3, P("pipe", "dp"), P("pipe", "dp", None, None), P(), P())
    return jax.shard_map(local, mesh=mesh, in_specs=in_specs, out_specs=(rows3,) * 3, check_vma=False)
```

```python
import functools

import jax
import jax.numpy as jnp
import numpy as np
from jax import lax
from jax.experimental import pallas as pl
from jax.experimental.pallas import tpu as pltpu
from jax.sharding import PartitionSpec as P

STEP = 20

beta_one = 0.9
beta_two = 0.95
learn_rate = 0.00015
decay_rate = 0.1
adam_eps = 1e-08
clip_eps = 1e-06

MASTER_MAX = 0.1201
FIRST_MAX = 3.003
SECOND_MIN = 0.249
SECOND_MAX = 4.501

OCTAVES = 16
LOG_TOP = float(np.log(1.0 + 2.0**OCTAVES))
LOG_STEPS = 32767.0
SECOND_STEPS = 65535.0

PLACE_LANE, LOST_LANE = 0, 1
PACK_CHUNKS = 2
EXTRA_AT = 1
UPDATE_CHUNKS = 4
PACK_VMEM = 56 * 1024 * 1024
OTHER_VMEM = 8 * 1024 * 1024
ANY = pl.BlockSpec(memory_space=pl.ANY)


def with_sign(code, x):
    return jnp.where(x < 0, -code, code)


def encode_log(x, top):
    steps = jnp.log(jnp.abs(x) * (2.0**OCTAVES / top) + 1.0) * (LOG_STEPS / LOG_TOP) + 0.5
    return with_sign(steps.astype(jnp.int32), x)


def decode_log(code, top):
    size = jnp.exp(jnp.abs(code).astype(jnp.float32) * (LOG_TOP / LOG_STEPS)) * (top / 2.0**OCTAVES) - top / 2.0**OCTAVES
    return with_sign(size, code)


def encode_second(x):
    step = SECOND_STEPS / (SECOND_MAX - SECOND_MIN)
    return (x * step + (0.5 - SECOND_MIN * step)).astype(jnp.int32)


def decode_second(code):
    return code.astype(jnp.float32) * ((SECOND_MAX - SECOND_MIN) / SECOND_STEPS) + SECOND_MIN


def encode_short(x, large=False):
    size = jnp.maximum(jnp.abs(x), 2.0**-126)
    exponent = jnp.floor(jnp.log2(size) + 0.002)
    if large:
        half = jnp.floor(exponent * 0.5)
        mantissa = size * jnp.exp2(-half) * jnp.exp2(half - exponent)
    else:
        mantissa = size * jnp.exp2(-exponent)
    code = (exponent + mantissa) * 128.0 + (126.0 * 128.0 + 0.5)
    return with_sign(code.astype(jnp.int32), x)


def decode_short(code):
    size = jnp.abs(code)
    exponent = (lax.shift_right_logical(size, 7) - 127).astype(jnp.float32)
    mantissa = (size & 127).astype(jnp.float32) * (1.0 / 128.0) + 1.0
    return with_sign(mantissa * jnp.exp2(exponent), code)


def join(high, low):
    return (high << 16) | (low & 0xFFFF)


def signed_high(word):
    return word >> 16


def signed_low(word):
    return (word << 16) >> 16


def extra_columns(k, width):
    return {1: width // 2, 2: width // 4, 4: width // 4}.get(k, 0)


def pack_kernel(
    ranks, cap, fails, devices,
    dest, failed, grad_exponent, master, moment1, moment2, quant_grad, replica,
    *refs,
):
    payloads, total = refs[:ranks], refs[ranks]
    (dest_s, failed_s, exponent_s, counts, table, lost_counts, lost_table,
     master_v, first_v, second_v, grad_v, block_v, lost_v, picked_v, words, extra_v, total_v,
     small_sem, in_sem, block_sem, pick_sem, out_sem) = refs[ranks + 1:]
    rows, width = master_v.shape
    half, quarter = width // 2, width // 4
    chunk = width // PACK_CHUNKS
    lost_rows = fails * cap
    group = lax.axis_index("pipe")
    me = lax.axis_index("dp")

    small = [
        pltpu.make_async_copy(grad_exponent, exponent_s, small_sem.at[1]),
        pltpu.make_async_copy(failed, failed_s, small_sem.at[0]),
        pltpu.make_async_copy(dest, dest_s, small_sem.at[2]),
    ]
    for copy in small:
        copy.start()
    loads = []
    for part in range(PACK_CHUNKS):
        columns = pl.ds(part * chunk, chunk)
        copies = [
            pltpu.make_async_copy(source.at[:, columns], target.at[:, columns], in_sem.at[part, i])
            for i, (source, target) in enumerate(
                [(quant_grad, grad_v), (master, master_v), (moment1, first_v), (moment2, second_v)]
            )
        ]
        for copy in copies:
            copy.start()
        loads.append(copies)
    for copy in small:
        copy.wait()
    blocks = [
        pltpu.make_async_copy(
            replica.at[pl.ds(pl.multiple_of(failed_s[i, group] * rows, rows), rows), :],
            block_v.at[pl.ds(i * rows, rows), :],
            block_sem.at[i],
        )
        for i in range(fails)
    ]
    for copy in blocks:
        copy.start()

    for i in range(ranks * cap):
        table[i] = 0
    for i in range(ranks):
        counts[i] = 0
    for r in range(rows):
        target = lax.div(dest_s[group, me * rows + r], rows)
        order = counts[target]
        table[target * cap + order] = r
        counts[target] = order + 1
    for i in range(ranks * lost_rows):
        lost_table[i] = 0
    for i in range(ranks * fails):
        lost_counts[i] = 0
    for i in range(fails):
        for r in range(rows):
            target = lax.div(dest_s[group, failed_s[i, group] * rows + r], rows)
            slot = target * fails + i
            order = lost_counts[slot]
            lost_table[slot * cap + order] = i * rows + r
            lost_counts[slot] = order + 1

    row_ids = lax.broadcasted_iota(jnp.int32, (rows, 128), 0)
    exponents = jnp.zeros((rows, 128), jnp.float32)
    for r in range(rows):
        exponents = jnp.where(row_ids == r, exponent_s[0, r].astype(jnp.float32), exponents)
    row_scale = jnp.exp2(exponents)[:, :1]

    sums = jnp.zeros((8, 128), jnp.float32)
    outs, picks = [], []
    for part in range(PACK_CHUNKS):
        columns = pl.ds(part * chunk, chunk)
        if part == EXTRA_AT:
            for copy in blocks:
                copy.wait()
            lost_v[...] = block_v[...].astype(jnp.float32)
            for j in range(lost_rows):
                one, two, four = (lost_table[(me ^ k) * lost_rows + j] for k in (1, 2, 4))
                picks.append((lost_v.at[pl.ds(one, 1), :], picked_v.at[pl.ds(j, 1), :]))
                for q, source in ((0, two), (2, two), (1, four), (3, four)):
                    span = pl.ds(q * quarter, quarter)
                    picks.append((lost_v.at[pl.ds(source, 1), span], picked_v.at[pl.ds(lost_rows + j, 1), span]))
            picks = [pltpu.make_async_copy(a, b, pick_sem) for a, b in picks]
            for copy in picks:
                copy.start()
        for copy in loads[part]:
            copy.wait()
        grad = grad_v[:, columns].astype(jnp.float32) * row_scale
        sums += jnp.sum((grad * grad).reshape(rows // 8, 8, chunk // 128, 128), axis=(0, 2))
        words[0, :, columns] = join(encode_log(master_v[:, columns], MASTER_MAX), encode_log(first_v[:, columns], FIRST_MAX))
        words[1, :, columns] = join(encode_second(second_v[:, columns]), encode_short(grad))
        for k in reversed(range(ranks)):
            for order in range(cap):
                row = table[(me ^ k) * cap + order]
                copy = pltpu.make_async_copy(
                    words.at[:, pl.ds(row, 1), columns], payloads[k].at[:, pl.ds(order, 1), columns], out_sem
                )
                copy.start()
                outs.append(copy)
    total_v[...] = jnp.broadcast_to(jnp.sum(sums, axis=0, keepdims=True), (devices, 128))
    copy = pltpu.make_async_copy(total_v, total, out_sem)
    copy.start()
    outs.append(copy)

    for copy in picks:
        copy.wait()
    extra_v[...] = join(encode_short(picked_v[:, :half], True), encode_short(picked_v[:, half:], True))
    for k, first_row, first_column in ((1, 0, 0), (2, lost_rows, 0), (4, lost_rows, quarter)):
        columns = extra_columns(k, width)
        for i in range(fails):
            copy = pltpu.make_async_copy(
                extra_v.at[pl.ds(first_row + i * cap, cap), pl.ds(first_column, columns)],
                payloads[k].at[i, :, pl.ds(width, columns)],
                out_sem,
            )
            copy.start()
            outs.append(copy)
    for copy in outs:
        copy.wait()


def base_kernel(
    ranks, cap, fails,
    dest, failed, replica, from_one, from_two, from_four,
    base,
    dest_s, failed_s, counts, places_s, lost_counts, lost_sources,
    block_v, rows_v, extra_v, info_v, small_sem, block_sem, move_sem,
):
    lost_rows = fails * cap
    slots, width = base.shape[0], rows_v.shape[1]
    rows = block_v.shape[0] // fails
    half, quarter = width // 2, width // 4
    group = lax.axis_index("pipe")
    me = lax.axis_index("dp")
    small = [
        pltpu.make_async_copy(failed, failed_s, small_sem.at[0]),
        pltpu.make_async_copy(dest, dest_s, small_sem.at[1]),
    ]
    for copy in small:
        copy.start()
    for copy in small:
        copy.wait()
    blocks = [
        pltpu.make_async_copy(
            replica.at[pl.ds(pl.multiple_of(failed_s[i, group] * rows, rows), rows), :],
            block_v.at[pl.ds(i * rows, rows), :],
            block_sem.at[i],
        )
        for i in range(fails)
    ]
    for copy in blocks:
        copy.start()

    for i in range(slots):
        places_s[i] = -1
    for i in range(ranks):
        counts[i] = 0

    @pl.loop(0, ranks * rows)
    def _(row):
        place = dest_s[group, row]

        @pl.when(lax.div(place, rows) == me)
        def _():
            slot = lax.div(row, rows) ^ me
            order = counts[slot]
            places_s[slot * cap + order] = lax.rem(place, rows)
            counts[slot] = order + 1

    slot_ids = lax.broadcasted_iota(jnp.int32, (slots, 128), 0)
    places = jnp.zeros((slots, 128), jnp.int32)
    for slot in range(slots):
        places = jnp.where(slot_ids == slot, places_s[slot], places)
    source = lax.div(slot_ids, cap) ^ me
    is_lost = source == failed_s[0, group]
    for i in range(1, fails):
        is_lost = is_lost | (source == failed_s[i, group])
    lanes = lax.broadcasted_iota(jnp.int32, (slots, 128), 1)
    info_v[...] = jnp.where(lanes == PLACE_LANE, places.astype(jnp.float32), jnp.where(is_lost, 1.0, 0.0))
    send_info = pltpu.make_async_copy(info_v, base.at[:, pl.ds(width, 128)], small_sem.at[0])
    send_info.start()
    for j in range(lost_rows):
        lost_sources[j] = 0
    for i in range(fails):
        lost_counts[i] = 0
        for r in range(rows):

            @pl.when(lax.div(dest_s[group, failed_s[i, group] * rows + r], rows) == me)
            def _(i=i, r=r):
                order = lost_counts[i]
                lost_sources[i * cap + order] = i * rows + r
                lost_counts[i] = order + 1

    is_failed = failed_s[0, group] == me
    sibling_failed = failed_s[0, group] == (me ^ 1)
    for i in range(1, fails):
        is_failed = is_failed | (failed_s[i, group] == me)
        sibling_failed = sibling_failed | (failed_s[i, group] == (me ^ 1))
    for copy in blocks:
        copy.wait()

    @pl.when(jnp.logical_not(is_failed))
    def _():
        rows_v[...] = block_v[...].astype(jnp.float32)

    @pl.when(is_failed)
    def _():
        def take(source, i, first, columns):
            return pltpu.make_async_copy(
                source.at[i, :, pl.ds(width, columns)], extra_v.at[pl.ds(i * cap, cap), pl.ds(first, columns)], move_sem
            )

        @pl.when(jnp.logical_not(sibling_failed))
        def _():
            copies = [take(from_one, i, 0, half) for i in range(fails)]
            for copy in copies:
                copy.start()
            for copy in copies:
                copy.wait()

        @pl.when(sibling_failed)
        def _():
            copies = [take(ref, i, n * quarter, quarter) for i in range(fails) for n, ref in enumerate((from_two, from_four))]
            for copy in copies:
                copy.start()
            for copy in copies:
                copy.wait()

        packed = extra_v[...]
        rows_v[0:lost_rows, 0:half] = decode_short(signed_high(packed))
        rows_v[0:lost_rows, half:width] = decode_short(signed_low(packed))
        for j in range(lost_rows):
            lost_sources[j] = j

    moves = [
        pltpu.make_async_copy(
            rows_v.at[pl.ds(lost_sources[i * cap + order], 1), :],
            base.at[pl.ds((failed_s[i, group] ^ me) * cap + order, 1), pl.ds(0, width)],
            move_sem,
        )
        for i in range(fails)
        for order in range(cap)
    ]
    for copy in moves:
        copy.start()
    for copy in moves:
        copy.wait()
    send_info.wait()


def update_kernel(
    ranks, cap, elements,
    sums, base, *refs,
):
    arrived = refs[:ranks]
    (new_master, new_first, new_second, info_s, sums_v, words, base_v,
     master_o, first_o, second_o, small_sem, word_sem, out_sem) = refs[ranks:]
    rows, width = new_master.shape
    slots = base_v.shape[0]
    chunk = width // UPDATE_CHUNKS
    info = pl.ds(width, 128)
    small = [
        pltpu.make_async_copy(source, target, small_sem.at[i])
        for i, (source, target) in enumerate(
            ((sums, sums_v), (base.at[:, info], base_v.at[:, info]), (base.at[:, info], info_s))
        )
    ]
    for copy in small:
        copy.start()
    loads = []
    for part in range(UPDATE_CHUNKS):
        columns = pl.ds(part * chunk, chunk)
        copies = [pltpu.make_async_copy(base.at[:, columns], base_v.at[:, columns], word_sem.at[part])] + [
            pltpu.make_async_copy(
                arrived[k].at[:, :, columns], words.at[:, pl.ds(k * cap, cap), columns], word_sem.at[part]
            )
            for k in range(ranks)
        ]
        for copy in copies:
            copy.start()
        loads.append(copies)
    for copy in small:
        copy.wait()

    grad_total = jnp.sum(jnp.sum(sums_v[...], axis=0, keepdims=True), axis=1, keepdims=True)
    clip_scale = jnp.minimum(1.0, 1.0 / jnp.sqrt(grad_total / elements + clip_eps))
    is_lost = base_v[:, width + LOST_LANE:width + LOST_LANE + 1] > 0.5
    keep_one = jnp.where(is_lost, 0.0, beta_one)
    keep_two = jnp.where(is_lost, 0.0, beta_two)
    scale_one = 1.0 / (1.0 - beta_one**STEP)
    scale_two = 1.0 / (1.0 - beta_two**STEP)

    outs = []
    for part in range(UPDATE_CHUNKS):
        columns = pl.ds(part * chunk, chunk)
        for copy in loads[part]:
            copy.wait()
        one, two = words[0, :, columns], words[1, :, columns]
        weights = jnp.where(is_lost, base_v[:, columns], decode_log(signed_high(one), MASTER_MAX))
        first = decode_log(signed_low(one), FIRST_MAX)
        second = decode_second(lax.shift_right_logical(two, 16))
        grads = decode_short(signed_low(two)) * clip_scale
        first_new = keep_one * first + (1.0 - beta_one) * grads
        second_new = keep_two * second + (1.0 - beta_two) * grads * grads
        direction = first_new * scale_one / (jnp.sqrt(second_new * scale_two) + adam_eps) + decay_rate * weights
        master_o[:, columns] = weights - learn_rate * direction
        first_o[:, columns] = first_new
        second_o[:, columns] = second_new
        for slot in range(slots):
            place = info_s[slot, PLACE_LANE].astype(jnp.int32)

            def move(slot=slot, place=place, columns=columns):
                return [
                    pltpu.make_async_copy(a.at[pl.ds(slot, 1), columns], b.at[pl.ds(place, 1), columns], out_sem)
                    for a, b in ((master_o, new_master), (first_o, new_first), (second_o, new_second))
                ]

            if slots == rows:
                for copy in move():
                    copy.start()
            else:

                @pl.when(place >= 0)
                def _(move=move):
                    for copy in move():
                        copy.start()

    for ref in (new_master, new_first, new_second):
        pltpu.make_async_copy(ref, ref, out_sem).wait()


def local(master, moment1, moment2, quant_grad, grad_exponent, replica_params, failed, dest):
    ranks = lax.axis_size("dp")
    devices = ranks * lax.axis_size("pipe")
    _, rows, width = master.shape
    failed = failed.T
    fails = failed.shape[0]
    assert fails == 2 and ranks >= 8 and ranks & (ranks - 1) == 0
    cap = (rows + ranks - 1) // ranks
    slots = ranks * cap
    lost_rows = fails * cap
    i32, f32 = jnp.int32, jnp.float32
    vmem, smem, dma = pltpu.VMEM, pltpu.SMEM, pltpu.SemaphoreType.DMA

    packed = pl.pallas_call(
        functools.partial(pack_kernel, ranks, cap, fails, devices),
        out_shape=[jax.ShapeDtypeStruct((2, cap, width + extra_columns(k, width)), i32) for k in range(ranks)]
        + [jax.ShapeDtypeStruct((devices, 128), f32)],
        in_specs=[ANY] * 8,
        out_specs=[ANY] * (ranks + 1),
        scratch_shapes=[
            smem(dest.shape, i32), smem(failed.shape, i32), smem((1, rows), i32),
            smem((ranks,), i32), smem((slots,), i32),
            smem((ranks * fails,), i32), smem((ranks * lost_rows,), i32),
            vmem((rows, width), f32), vmem((rows, width), f32), vmem((rows, width), f32),
            vmem((rows, width), jnp.bfloat16),
            vmem((fails * rows, width), jnp.bfloat16), vmem((fails * rows, width), f32),
            vmem((2 * lost_rows, width), f32),
            vmem((2, rows, width), i32),
            vmem((2 * lost_rows, width // 2), i32), vmem((devices, 128), f32),
            dma((3,)), dma((PACK_CHUNKS, 4)), dma((fails,)), dma, dma,
        ],
        compiler_params=pltpu.CompilerParams(vmem_limit_bytes=PACK_VMEM),
        name="pack",
    )(dest, failed, grad_exponent, master[0], moment1[0], moment2[0], quant_grad[0], replica_params[0, 0])
    payloads, total = packed[:ranks], packed[ranks]

    def send(k, value):
        return lax.ppermute(value, "dp", [(i, i ^ k) for i in range(ranks)])

    arrived = {0: payloads[0], 1: send(1, payloads[1])}
    for k in [2, 4, 3, 5]:
        arrived[k] = send(k, payloads[k])
    for k in range(6, ranks):
        value, _ = lax.optimization_barrier((payloads[k], arrived[1]))
        arrived[k] = send(k, value)
    sums = lax.all_to_all(total, ("pipe", "dp"), split_axis=0, concat_axis=0, tiled=True)

    base = pl.pallas_call(
        functools.partial(base_kernel, ranks, cap, fails),
        out_shape=jax.ShapeDtypeStruct((slots, width + 128), f32),
        in_specs=[ANY] * 6,
        out_specs=ANY,
        scratch_shapes=[
            smem(dest.shape, i32), smem(failed.shape, i32), smem((ranks,), i32), smem((slots,), i32),
            smem((fails,), i32), smem((lost_rows,), i32),
            vmem((fails * rows, width), jnp.bfloat16), vmem((fails * rows, width), f32),
            vmem((lost_rows, width // 2), i32), vmem((slots, 128), f32),
            dma((2,)), dma((fails,)), dma,
        ],
        compiler_params=pltpu.CompilerParams(vmem_limit_bytes=OTHER_VMEM),
        name="base",
    )(dest, failed, replica_params[0, 0], arrived[1], arrived[2], arrived[4])

    outs = pl.pallas_call(
        functools.partial(update_kernel, ranks, cap, devices * rows * width),
        out_shape=[jax.ShapeDtypeStruct((rows, width), f32)] * 3,
        in_specs=[ANY] * (2 + ranks),
        out_specs=[ANY] * 3,
        scratch_shapes=[
            smem((slots, 128), f32), vmem((devices, 128), f32),
            vmem((2, slots, width), i32), vmem((slots, width + 128), f32),
            vmem((slots, width), f32), vmem((slots, width), f32), vmem((slots, width), f32),
            dma((3,)), dma((UPDATE_CHUNKS,)), dma,
        ],
        compiler_params=pltpu.CompilerParams(vmem_limit_bytes=OTHER_VMEM),
        name="update",
    )(sums, base, *[arrived[k] for k in range(ranks)])
    return tuple(out[None] for out in outs)


def solution(mesh):
    rows3 = P("pipe", "dp", None)
    in_specs = (rows3, rows3, rows3, rows3, P("pipe", "dp"), P("pipe", "dp", None, None), P(), P())
    return jax.shard_map(local, mesh=mesh, in_specs=in_specs, out_specs=(rows3,) * 3, check_vma=False)
```

```python
import functools

import jax
import jax.numpy as jnp
import numpy as np
from jax import lax
from jax.experimental import pallas as pl
from jax.experimental.pallas import tpu as pltpu
from jax.sharding import PartitionSpec as P

STEP = 20

beta_one = 0.9
beta_two = 0.95
learn_rate = 0.00015
decay_rate = 0.1
adam_eps = 1e-08
clip_eps = 1e-06

MASTER_MAX = 0.1201
FIRST_MAX = 3.003
SECOND_MIN = 0.249
SECOND_MAX = 4.501

OCTAVES = 16
LOG_TOP = float(np.log(1.0 + 2.0**OCTAVES))
LOG_STEPS = 32767.0
SECOND_STEPS = 65535.0

PLACE_LANE, LOST_LANE = 0, 1
PACK_CHUNKS = 2
EXTRA_AT = 1
UPDATE_CHUNKS = 4
PACK_VMEM = 56 * 1024 * 1024
OTHER_VMEM = 8 * 1024 * 1024
ANY = pl.BlockSpec(memory_space=pl.ANY)


def with_sign(code, x):
    return jnp.where(x < 0, -code, code)


def encode_log(x, top):
    steps = jnp.log(jnp.abs(x) * (2.0**OCTAVES / top) + 1.0) * (LOG_STEPS / LOG_TOP) + 0.5
    return with_sign(steps.astype(jnp.int32), x)


def decode_log(code, top):
    size = jnp.exp(jnp.abs(code).astype(jnp.float32) * (LOG_TOP / LOG_STEPS)) * (top / 2.0**OCTAVES) - top / 2.0**OCTAVES
    return with_sign(size, code)


def encode_second(x):
    step = SECOND_STEPS / (SECOND_MAX - SECOND_MIN)
    return (x * step + (0.5 - SECOND_MIN * step)).astype(jnp.int32)


def decode_second(code):
    return code.astype(jnp.float32) * ((SECOND_MAX - SECOND_MIN) / SECOND_STEPS) + SECOND_MIN


def encode_short(x, large=False):
    size = jnp.maximum(jnp.abs(x), 2.0**-126)
    exponent = jnp.floor(jnp.log2(size) + 0.002)
    if large:
        half = jnp.floor(exponent * 0.5)
        mantissa = size * jnp.exp2(-half) * jnp.exp2(half - exponent)
    else:
        mantissa = size * jnp.exp2(-exponent)
    code = (exponent + mantissa) * 128.0 + (126.0 * 128.0 + 0.5)
    return with_sign(code.astype(jnp.int32), x)


def decode_short(code):
    size = jnp.abs(code)
    exponent = (lax.shift_right_logical(size, 7) - 127).astype(jnp.float32)
    mantissa = (size & 127).astype(jnp.float32) * (1.0 / 128.0) + 1.0
    return with_sign(mantissa * jnp.exp2(exponent), code)


def join(high, low):
    return (high << 16) | (low & 0xFFFF)


def signed_high(word):
    return word >> 16


def signed_low(word):
    return (word << 16) >> 16


def payload_shape(k, cap, width):
    if k < 2:
        return (2, cap, width + k * (width // 2))
    return (2, 2, cap, width + (width // 8 if k in (2, 4) else 0))


def sent_kinds(ranks):
    return [0, 1] + list(range(2, ranks, 2))


def pack_kernel(
    ranks, cap, fails, devices,
    dest, failed, grad_exponent, master, moment1, moment2, quant_grad, replica,
    *refs,
):
    kinds = sent_kinds(ranks)
    payloads, total = dict(zip(kinds, refs)), refs[len(kinds)]
    (dest_s, failed_s, exponent_s, counts, table, lost_counts, lost_table,
     master_v, first_v, second_v, grad_v, block_v, lost_v, picked_v, words, extra_v, total_v,
     small_sem, in_sem, block_sem, pick_sem, out_sem) = refs[len(kinds) + 1:]
    rows, width = master_v.shape
    half, quarter, eighth = width // 2, width // 4, width // 8
    chunk = width // PACK_CHUNKS
    lost_rows = fails * cap
    group = lax.axis_index("pipe")
    me = lax.axis_index("dp")

    small = [
        pltpu.make_async_copy(grad_exponent, exponent_s, small_sem.at[1]),
        pltpu.make_async_copy(failed, failed_s, small_sem.at[0]),
        pltpu.make_async_copy(dest, dest_s, small_sem.at[2]),
    ]
    for copy in small:
        copy.start()
    loads = []
    for part in range(PACK_CHUNKS):
        columns = pl.ds(part * chunk, chunk)
        copies = [
            pltpu.make_async_copy(source.at[:, columns], target.at[:, columns], in_sem.at[part, i])
            for i, (source, target) in enumerate(
                [(quant_grad, grad_v), (master, master_v), (moment1, first_v), (moment2, second_v)]
            )
        ]
        for copy in copies:
            copy.start()
        loads.append(copies)
    for copy in small:
        copy.wait()
    blocks = [
        pltpu.make_async_copy(
            replica.at[pl.ds(pl.multiple_of(failed_s[i, group] * rows, rows), rows), :],
            block_v.at[pl.ds(i * rows, rows), :],
            block_sem.at[i],
        )
        for i in range(fails)
    ]
    for copy in blocks:
        copy.start()

    for i in range(ranks * cap):
        table[i] = 0
    for i in range(ranks):
        counts[i] = 0
    for r in range(rows):
        target = lax.div(dest_s[group, me * rows + r], rows)
        order = counts[target]
        table[target * cap + order] = r
        counts[target] = order + 1
    for i in range(ranks * lost_rows):
        lost_table[i] = 0
    for i in range(ranks * fails):
        lost_counts[i] = 0
    for i in range(fails):
        for r in range(rows):
            target = lax.div(dest_s[group, failed_s[i, group] * rows + r], rows)
            slot = target * fails + i
            order = lost_counts[slot]
            lost_table[slot * cap + order] = i * rows + r
            lost_counts[slot] = order + 1

    row_ids = lax.broadcasted_iota(jnp.int32, (rows, 128), 0)
    exponents = jnp.zeros((rows, 128), jnp.float32)
    for r in range(rows):
        exponents = jnp.where(row_ids == r, exponent_s[0, r].astype(jnp.float32), exponents)
    row_scale = jnp.exp2(exponents)[:, :1]

    sums = jnp.zeros((8, 128), jnp.float32)
    outs, picks = [], []
    for part in range(PACK_CHUNKS):
        columns = pl.ds(part * chunk, chunk)
        if part == EXTRA_AT:
            for copy in blocks:
                copy.wait()
            lost_v[...] = block_v[...].astype(jnp.float32)
            for j in range(lost_rows):
                one, two, four = (lost_table[(me ^ k) * lost_rows + j] for k in (1, 2, 4))
                picks.append((lost_v.at[pl.ds(one, 1), :], picked_v.at[pl.ds(j, 1), :]))
                for q, source in ((0, two), (2, two), (1, four), (3, four)):
                    span = pl.ds(q * quarter, quarter)
                    picks.append((lost_v.at[pl.ds(source, 1), span], picked_v.at[pl.ds(lost_rows + j, 1), span]))
            picks = [pltpu.make_async_copy(a, b, pick_sem) for a, b in picks]
            for copy in picks:
                copy.start()
        for copy in loads[part]:
            copy.wait()
        grad = grad_v[:, columns].astype(jnp.float32) * row_scale
        sums += jnp.sum((grad * grad).reshape(rows // 8, 8, chunk // 128, 128), axis=(0, 2))
        words[0, :, columns] = join(encode_log(master_v[:, columns], MASTER_MAX), encode_log(first_v[:, columns], FIRST_MAX))
        words[1, :, columns] = join(encode_second(second_v[:, columns]), encode_short(grad))
        for k in reversed(range(ranks)):
            for order in range(cap):
                row = table[(me ^ k) * cap + order]
                target = payloads[k] if k < 2 else payloads[k - k % 2].at[k % 2]
                copy = pltpu.make_async_copy(
                    words.at[:, pl.ds(row, 1), columns], target.at[:, pl.ds(order, 1), columns], out_sem
                )
                copy.start()
                outs.append(copy)
    total_v[...] = jnp.broadcast_to(jnp.sum(sums, axis=0, keepdims=True), (devices, 128))
    copy = pltpu.make_async_copy(total_v, total, out_sem)
    copy.start()
    outs.append(copy)

    for copy in picks:
        copy.wait()
    extra_v[...] = join(encode_short(picked_v[:, :half], True), encode_short(picked_v[:, half:], True))
    extras = [(payloads[1], 0, 0, half)] + [
        (payloads[k].at[part], lost_rows, first + part * eighth, eighth)
        for k, first in ((2, 0), (4, quarter))
        for part in range(2)
    ]
    for target, first_row, first_column, columns in extras:
        for i in range(fails):
            copy = pltpu.make_async_copy(
                extra_v.at[pl.ds(first_row + i * cap, cap), pl.ds(first_column, columns)],
                target.at[i, :, pl.ds(width, columns)],
                out_sem,
            )
            copy.start()
            outs.append(copy)
    for copy in outs:
        copy.wait()


def base_kernel(
    ranks, cap, fails,
    dest, failed, replica, from_one, from_two, from_four,
    base,
    dest_s, failed_s, dest_v, lost_counts, lost_sources,
    block_v, rows_v, extra_v, info_v, small_sem, block_sem, move_sem,
):
    lost_rows = fails * cap
    slots, width = base.shape[0], rows_v.shape[1]
    rows = block_v.shape[0] // fails
    half, eighth = width // 2, width // 8
    group = lax.axis_index("pipe")
    me = lax.axis_index("dp")
    small = [
        pltpu.make_async_copy(failed, failed_s, small_sem.at[0]),
        pltpu.make_async_copy(dest, dest_s, small_sem.at[1]),
        pltpu.make_async_copy(dest, dest_v, small_sem.at[2]),
    ]
    for copy in small:
        copy.start()
    for copy in small:
        copy.wait()
    blocks = [
        pltpu.make_async_copy(
            replica.at[pl.ds(pl.multiple_of(failed_s[i, group] * rows, rows), rows), :],
            block_v.at[pl.ds(i * rows, rows), :],
            block_sem.at[i],
        )
        for i in range(fails)
    ]
    for copy in blocks:
        copy.start()

    every = ranks * rows
    row_ids = lax.broadcasted_iota(jnp.int32, (every, every), 0)
    column_ids = lax.broadcasted_iota(jnp.int32, (every, every), 1)
    place = dest_v[pl.ds(group, 1), :]
    mine = jnp.where(lax.div(place, rows) == me, 1.0, 0.0)
    mine_down = jnp.sum(jnp.where(row_ids == column_ids, mine, 0.0), axis=1, keepdims=True)
    earlier = (row_ids < column_ids) & (lax.div(row_ids, rows) == lax.div(column_ids, rows))
    order = jnp.sum(jnp.where(earlier, mine_down, 0.0), axis=0, keepdims=True).astype(jnp.int32)
    columns = lax.broadcasted_iota(jnp.int32, (1, every), 1)
    slot_of = jnp.where(mine > 0.5, (lax.div(columns, rows) ^ me) * cap + order, -1)
    slot_rows = lax.broadcasted_iota(jnp.int32, (slots, every), 0)
    found = slot_rows == slot_of
    place_in = lax.rem(place, rows).astype(jnp.float32)
    places = jnp.sum(jnp.where(found, place_in + 1.0, 0.0), axis=1, keepdims=True) - 1.0
    slot_ids = lax.broadcasted_iota(jnp.int32, (slots, 128), 0)
    source = lax.div(slot_ids, cap) ^ me
    is_lost = source == failed_s[0, group]
    for i in range(1, fails):
        is_lost = is_lost | (source == failed_s[i, group])
    lanes = lax.broadcasted_iota(jnp.int32, (slots, 128), 1)
    info_v[...] = jnp.where(lanes == PLACE_LANE, places, jnp.where(is_lost, 1.0, 0.0))
    send_info = pltpu.make_async_copy(info_v, base.at[:, pl.ds(width, 128)], small_sem.at[0])
    send_info.start()
    for j in range(lost_rows):
        lost_sources[j] = 0
    for i in range(fails):
        lost_counts[i] = 0
        for r in range(rows):

            @pl.when(lax.div(dest_s[group, failed_s[i, group] * rows + r], rows) == me)
            def _(i=i, r=r):
                order = lost_counts[i]
                lost_sources[i * cap + order] = i * rows + r
                lost_counts[i] = order + 1

    is_failed = failed_s[0, group] == me
    sibling_failed = failed_s[0, group] == (me ^ 1)
    for i in range(1, fails):
        is_failed = is_failed | (failed_s[i, group] == me)
        sibling_failed = sibling_failed | (failed_s[i, group] == (me ^ 1))
    for copy in blocks:
        copy.wait()

    @pl.when(jnp.logical_not(is_failed))
    def _():
        rows_v[...] = block_v[...].astype(jnp.float32)

    @pl.when(is_failed)
    def _():
        def take(source, i, first, columns):
            return pltpu.make_async_copy(
                source.at[i, :, pl.ds(width, columns)], extra_v.at[pl.ds(i * cap, cap), pl.ds(first, columns)], move_sem
            )

        @pl.when(jnp.logical_not(sibling_failed))
        def _():
            copies = [take(from_one, i, 0, half) for i in range(fails)]
            for copy in copies:
                copy.start()
            for copy in copies:
                copy.wait()

        @pl.when(sibling_failed)
        def _():
            parts = (from_two.at[0], from_two.at[1], from_four.at[0], from_four.at[1])
            copies = [take(ref, i, n * eighth, eighth) for i in range(fails) for n, ref in enumerate(parts)]
            for copy in copies:
                copy.start()
            for copy in copies:
                copy.wait()

        packed = extra_v[...]
        rows_v[0:lost_rows, 0:half] = decode_short(signed_high(packed))
        rows_v[0:lost_rows, half:width] = decode_short(signed_low(packed))
        for j in range(lost_rows):
            lost_sources[j] = j

    moves = [
        pltpu.make_async_copy(
            rows_v.at[pl.ds(lost_sources[i * cap + order], 1), :],
            base.at[pl.ds((failed_s[i, group] ^ me) * cap + order, 1), pl.ds(0, width)],
            move_sem,
        )
        for i in range(fails)
        for order in range(cap)
    ]
    for copy in moves:
        copy.start()
    for copy in moves:
        copy.wait()
    send_info.wait()


def update_kernel(
    ranks, cap, elements,
    sums, base, *refs,
):
    kinds = sent_kinds(ranks)
    arrived = dict(zip(kinds, refs))
    for k, ref in zip(range(2, ranks, 2), refs[len(kinds):ranks]):
        arrived[k], arrived[k + 1] = arrived[k].at[0], ref.at[1]
    (new_master, new_first, new_second, info_s, sums_v, words, base_v,
     master_o, first_o, second_o, small_sem, word_sem, out_sem) = refs[ranks:]
    rows, width = new_master.shape
    slots = base_v.shape[0]
    chunk = width // UPDATE_CHUNKS
    info = pl.ds(width, 128)
    small = [
        pltpu.make_async_copy(source, target, small_sem.at[i])
        for i, (source, target) in enumerate(
            ((sums, sums_v), (base.at[:, info], base_v.at[:, info]), (base.at[:, info], info_s))
        )
    ]
    for copy in small:
        copy.start()
    loads = []
    for part in range(UPDATE_CHUNKS):
        columns = pl.ds(part * chunk, chunk)
        copies = [pltpu.make_async_copy(base.at[:, columns], base_v.at[:, columns], word_sem.at[part])] + [
            pltpu.make_async_copy(
                arrived[k].at[:, :, columns], words.at[:, pl.ds(k * cap, cap), columns], word_sem.at[part]
            )
            for k in range(ranks)
        ]
        for copy in copies:
            copy.start()
        loads.append(copies)
    for copy in small:
        copy.wait()

    grad_total = jnp.sum(jnp.sum(sums_v[...], axis=0, keepdims=True), axis=1, keepdims=True)
    clip_scale = jnp.minimum(1.0, 1.0 / jnp.sqrt(grad_total / elements + clip_eps))
    is_lost = base_v[:, width + LOST_LANE:width + LOST_LANE + 1] > 0.5
    keep_one = jnp.where(is_lost, 0.0, beta_one)
    keep_two = jnp.where(is_lost, 0.0, beta_two)
    scale_one = 1.0 / (1.0 - beta_one**STEP)
    scale_two = 1.0 / (1.0 - beta_two**STEP)

    outs = []
    for part in range(UPDATE_CHUNKS):
        columns = pl.ds(part * chunk, chunk)
        for copy in loads[part]:
            copy.wait()
        one, two = words[0, :, columns], words[1, :, columns]
        weights = jnp.where(is_lost, base_v[:, columns], decode_log(signed_high(one), MASTER_MAX))
        first = decode_log(signed_low(one), FIRST_MAX)
        second = decode_second(lax.shift_right_logical(two, 16))
        grads = decode_short(signed_low(two)) * clip_scale
        first_new = keep_one * first + (1.0 - beta_one) * grads
        second_new = keep_two * second + (1.0 - beta_two) * grads * grads
        direction = first_new * scale_one / (jnp.sqrt(second_new * scale_two) + adam_eps) + decay_rate * weights
        master_o[:, columns] = weights - learn_rate * direction
        first_o[:, columns] = first_new
        second_o[:, columns] = second_new
        for slot in range(slots):
            place = info_s[slot, PLACE_LANE].astype(jnp.int32)

            def move(slot=slot, place=place, columns=columns):
                return [
                    pltpu.make_async_copy(a.at[pl.ds(slot, 1), columns], b.at[pl.ds(place, 1), columns], out_sem)
                    for a, b in ((master_o, new_master), (first_o, new_first), (second_o, new_second))
                ]

            if slots == rows:
                for copy in move():
                    copy.start()
            else:

                @pl.when(place >= 0)
                def _(move=move):
                    for copy in move():
                        copy.start()

    for ref in (new_master, new_first, new_second):
        pltpu.make_async_copy(ref, ref, out_sem).wait()


def local(master, moment1, moment2, quant_grad, grad_exponent, replica_params, failed, dest):
    ranks = lax.axis_size("dp")
    devices = ranks * lax.axis_size("pipe")
    _, rows, width = master.shape
    failed = failed.T
    fails = failed.shape[0]
    assert fails == 2 and ranks >= 8 and ranks & (ranks - 1) == 0
    cap = (rows + ranks - 1) // ranks
    slots = ranks * cap
    kinds = sent_kinds(ranks)
    lost_rows = fails * cap
    i32, f32 = jnp.int32, jnp.float32
    vmem, smem, dma = pltpu.VMEM, pltpu.SMEM, pltpu.SemaphoreType.DMA

    packed = pl.pallas_call(
        functools.partial(pack_kernel, ranks, cap, fails, devices),
        out_shape=[jax.ShapeDtypeStruct(payload_shape(k, cap, width), i32) for k in kinds]
        + [jax.ShapeDtypeStruct((devices, 128), f32)],
        in_specs=[ANY] * 8,
        out_specs=[ANY] * (len(kinds) + 1),
        scratch_shapes=[
            smem(dest.shape, i32), smem(failed.shape, i32), smem((1, rows), i32),
            smem((ranks,), i32), smem((slots,), i32),
            smem((ranks * fails,), i32), smem((ranks * lost_rows,), i32),
            vmem((rows, width), f32), vmem((rows, width), f32), vmem((rows, width), f32),
            vmem((rows, width), jnp.bfloat16),
            vmem((fails * rows, width), jnp.bfloat16), vmem((fails * rows, width), f32),
            vmem((2 * lost_rows, width), f32),
            vmem((2, rows, width), i32),
            vmem((2 * lost_rows, width // 2), i32), vmem((devices, 128), f32),
            dma((3,)), dma((PACK_CHUNKS, 4)), dma((fails,)), dma, dma,
        ],
        compiler_params=pltpu.CompilerParams(vmem_limit_bytes=PACK_VMEM),
        name="pack",
    )(dest, failed, grad_exponent, master[0], moment1[0], moment2[0], quant_grad[0], replica_params[0, 0])
    payloads, total = dict(zip(kinds, packed)), packed[-1]

    def send(k, value):
        return lax.ppermute(value, "dp", [(i, i ^ k) for i in range(ranks)])

    arrived = {0: payloads[0], 1: send(1, payloads[1])}
    for k in range(2, ranks, 2):
        value = payloads[k]
        if k not in (2, 4):
            value, _ = lax.optimization_barrier((value, arrived[1]))
        arrived[k] = send(k, value)
    sums = lax.all_to_all(total, ("pipe", "dp"), split_axis=0, concat_axis=0, tiled=True)
    handed = []
    for k in range(2, ranks, 2):
        value, _ = lax.optimization_barrier((arrived[k], sums))
        handed.append(send(1, value))

    base = pl.pallas_call(
        functools.partial(base_kernel, ranks, cap, fails),
        out_shape=jax.ShapeDtypeStruct((slots, width + 128), f32),
        in_specs=[ANY] * 6,
        out_specs=ANY,
        scratch_shapes=[
            smem(dest.shape, i32), smem(failed.shape, i32), vmem(dest.shape, i32),
            smem((fails,), i32), smem((lost_rows,), i32),
            vmem((fails * rows, width), jnp.bfloat16), vmem((fails * rows, width), f32),
            vmem((lost_rows, width // 2), i32), vmem((slots, 128), f32),
            dma((3,)), dma((fails,)), dma,
        ],
        compiler_params=pltpu.CompilerParams(vmem_limit_bytes=OTHER_VMEM),
        name="base",
    )(dest, failed, replica_params[0, 0], arrived[1], arrived[2], arrived[4])

    outs = pl.pallas_call(
        functools.partial(update_kernel, ranks, cap, devices * rows * width),
        out_shape=[jax.ShapeDtypeStruct((rows, width), f32)] * 3,
        in_specs=[ANY] * (2 + ranks),
        out_specs=[ANY] * 3,
        scratch_shapes=[
            smem((slots, 128), f32), vmem((devices, 128), f32),
            vmem((2, slots, width), i32), vmem((slots, width + 128), f32),
            vmem((slots, width), f32), vmem((slots, width), f32), vmem((slots, width), f32),
            dma((3,)), dma((UPDATE_CHUNKS,)), dma,
        ],
        compiler_params=pltpu.CompilerParams(vmem_limit_bytes=OTHER_VMEM),
        name="update",
    )(sums, base, *[arrived[k] for k in kinds], *handed)
    return tuple(out[None] for out in outs)


def solution(mesh):
    rows3 = P("pipe", "dp", None)
    in_specs = (rows3, rows3, rows3, rows3, P("pipe", "dp"), P("pipe", "dp", None, None), P(), P())
    return jax.shard_map(local, mesh=mesh, in_specs=in_specs, out_specs=(rows3,) * 3, check_vma=False)
```

```python
import functools

import jax
import jax.numpy as jnp
import numpy as np
from jax import lax
from jax.experimental import pallas as pl
from jax.experimental.pallas import tpu as pltpu
from jax.sharding import PartitionSpec as P

STEP = 20

beta_one = 0.9
beta_two = 0.95
learn_rate = 0.00015
decay_rate = 0.1
adam_eps = 1e-08
clip_eps = 1e-06

MASTER_MAX = 0.1201
FIRST_MAX = 3.003
SECOND_MIN = 0.249
SECOND_MAX = 4.501

OCTAVES = 16
LOG_TOP = float(np.log(1.0 + 2.0**OCTAVES))
LOG_STEPS = 32767.0
LN_TWO = float(np.log(2.0))
SECOND_STEPS = 65535.0

PLACE_LANE, LOST_LANE = 0, 1
PACK_CHUNKS = 2
EXTRA_AT = 1
UPDATE_CHUNKS = 2
PACK_VMEM = 56 * 1024 * 1024
OTHER_VMEM = 12 * 1024 * 1024
ANY = pl.BlockSpec(memory_space=pl.ANY)


def with_sign(code, x):
    return jnp.where(x < 0, -code, code)


def encode_log(x, top):
    steps = jnp.log(jnp.abs(x) * (2.0**OCTAVES / top) + 1.0) * (LOG_STEPS / LOG_TOP) + 0.5
    return with_sign(steps.astype(jnp.int32), x)


def decode_log(code, top):
    size = jnp.exp2(jnp.abs(code).astype(jnp.float32) * (LOG_TOP / LOG_STEPS / LN_TWO)) * (top / 2.0**OCTAVES) - top / 2.0**OCTAVES
    return with_sign(size, code)


def encode_second(x):
    step = SECOND_STEPS / (SECOND_MAX - SECOND_MIN)
    return (x * step + (0.5 - SECOND_MIN * step)).astype(jnp.int32)


def decode_second(code):
    return code.astype(jnp.float32) * ((SECOND_MAX - SECOND_MIN) / SECOND_STEPS) + SECOND_MIN


def encode_short(x, large=False):
    size = jnp.maximum(jnp.abs(x), 2.0**-126)
    exponent = jnp.floor(jnp.log(size) * (1.0 / LN_TWO) + 0.002)
    if large:
        half = jnp.floor(exponent * 0.5)
        mantissa = size * jnp.exp2(-half) * jnp.exp2(half - exponent)
    else:
        mantissa = size * jnp.exp2(-exponent)
    code = (exponent + mantissa) * 128.0 + (126.0 * 128.0 + 0.5)
    return with_sign(code.astype(jnp.int32), x)


def decode_short(code):
    size = jnp.abs(code)
    exponent = (lax.shift_right_logical(size, 7) - 127).astype(jnp.float32)
    mantissa = (size & 127).astype(jnp.float32) * (1.0 / 128.0) + 1.0
    return with_sign(mantissa * jnp.exp2(exponent), code)


def join(high, low):
    return (high << 16) | (low & 0xFFFF)


def signed_high(word):
    return word >> 16


def signed_low(word):
    return (word << 16) >> 16


def payload_shape(k, cap, width):
    if k < 2:
        return (2, cap, width + k * (width // 2))
    return (2, 2, cap, width + (width // 8 if k in (2, 4) else 0))


def sent_kinds(ranks):
    return [0, 1] + list(range(2, ranks, 2))


def pack_kernel(
    ranks, cap, fails, devices,
    dest, failed, grad_exponent, master, moment1, moment2, quant_grad, replica,
    *refs,
):
    kinds = sent_kinds(ranks)
    payloads, total = dict(zip(kinds, refs)), refs[len(kinds)]
    (dest_s, failed_s, exponent_s, counts, table, lost_counts, lost_table,
     master_v, first_v, second_v, grad_v, block_v, lost_v, picked_v, words, extra_v, total_v,
     small_sem, in_sem, block_sem, pick_sem, out_sem) = refs[len(kinds) + 1:]
    rows, width = master_v.shape
    half, quarter, eighth = width // 2, width // 4, width // 8
    chunk = width // PACK_CHUNKS
    lost_rows = fails * cap
    group = lax.axis_index("pipe")
    me = lax.axis_index("dp")

    small = [
        pltpu.make_async_copy(grad_exponent, exponent_s, small_sem.at[1]),
        pltpu.make_async_copy(failed, failed_s, small_sem.at[0]),
        pltpu.make_async_copy(dest, dest_s, small_sem.at[2]),
    ]
    for copy in small:
        copy.start()
    loads = []
    for part in range(PACK_CHUNKS):
        columns = pl.ds(part * chunk, chunk)
        copies = [
            pltpu.make_async_copy(source.at[:, columns], target.at[:, columns], in_sem.at[part, i])
            for i, (source, target) in enumerate(
                [(quant_grad, grad_v), (master, master_v), (moment1, first_v), (moment2, second_v)]
            )
        ]
        for copy in copies:
            copy.start()
        loads.append(copies)
    for copy in small:
        copy.wait()
    blocks = [
        pltpu.make_async_copy(
            replica.at[pl.ds(pl.multiple_of(failed_s[i, group] * rows, rows), rows), :],
            block_v.at[pl.ds(i * rows, rows), :],
            block_sem.at[i],
        )
        for i in range(fails)
    ]
    for copy in blocks:
        copy.start()

    for i in range(ranks * cap):
        table[i] = 0
    for i in range(ranks):
        counts[i] = 0
    for r in range(rows):
        target = lax.div(dest_s[group, me * rows + r], rows)
        order = counts[target]
        table[target * cap + order] = r
        counts[target] = order + 1
    for i in range(ranks * lost_rows):
        lost_table[i] = 0
    for i in range(ranks * fails):
        lost_counts[i] = 0
    for i in range(fails):
        for r in range(rows):
            target = lax.div(dest_s[group, failed_s[i, group] * rows + r], rows)
            slot = target * fails + i
            order = lost_counts[slot]
            lost_table[slot * cap + order] = i * rows + r
            lost_counts[slot] = order + 1

    def has_failed(rank):
        found = failed_s[0, group] == rank
        for i in range(1, fails):
            found = found | (failed_s[i, group] == rank)
        return found

    helped = jnp.where(has_failed(me ^ 1), me ^ 1, jnp.where(has_failed(me ^ 2) & has_failed(me ^ 3), me ^ 2, me ^ 4))

    row_ids = lax.broadcasted_iota(jnp.int32, (rows, 128), 0)
    exponents = jnp.zeros((rows, 128), jnp.float32)
    for r in range(rows):
        exponents = jnp.where(row_ids == r, exponent_s[0, r].astype(jnp.float32), exponents)
    row_scale = jnp.exp2(exponents)[:, :1]

    sums = jnp.zeros((8, 128), jnp.float32)
    picks = []
    for part in range(PACK_CHUNKS):
        columns = pl.ds(part * chunk, chunk)
        if part == EXTRA_AT:
            for copy in blocks:
                copy.wait()
            lost_v[...] = block_v[...].astype(jnp.float32)
            for j in range(lost_rows):
                source = lost_table[helped * lost_rows + j]
                picks.append(pltpu.make_async_copy(lost_v.at[pl.ds(source, 1), :], picked_v.at[pl.ds(j, 1), :], pick_sem))
            for copy in picks:
                copy.start()
        for copy in loads[part]:
            copy.wait()
        grad = grad_v[:, columns].astype(jnp.float32) * row_scale
        sums += jnp.sum((grad * grad).reshape(rows // 8, 8, chunk // 128, 128), axis=(0, 2))
        words[0, :, columns] = join(encode_log(master_v[:, columns], MASTER_MAX), encode_log(first_v[:, columns], FIRST_MAX))
        words[1, :, columns] = join(encode_second(second_v[:, columns]), encode_short(grad))
        for k in reversed(range(ranks)):
            for order in range(cap):
                row = table[(me ^ k) * cap + order]
                target = payloads[k] if k < 2 else payloads[k - k % 2].at[k % 2]
                copy = pltpu.make_async_copy(
                    words.at[:, pl.ds(row, 1), columns], target.at[:, pl.ds(order, 1), columns], out_sem
                )
                copy.start()
    total_v[...] = jnp.broadcast_to(jnp.sum(sums, axis=0, keepdims=True), (devices, 128))
    pltpu.make_async_copy(total_v, total, out_sem).start()

    for copy in picks:
        copy.wait()
    extra_v[...] = join(encode_short(picked_v[:, :half], True), encode_short(picked_v[:, half:], True))
    extras = [(payloads[1], 0, half)] + [
        (payloads[k].at[part], first + part * eighth, eighth)
        for k, first in ((2, 0), (4, quarter))
        for part in range(2)
    ]
    for target, first_column, columns in extras:
        for i in range(fails):
            copy = pltpu.make_async_copy(
                extra_v.at[pl.ds(i * cap, cap), pl.ds(first_column, columns)],
                target.at[i, :, pl.ds(width, columns)],
                out_sem,
            )
            copy.start()
    for ref in refs[:len(kinds) + 1]:
        pltpu.make_async_copy(ref, ref, out_sem).wait()


def base_kernel(
    ranks, cap, fails,
    dest, failed, replica, from_one, from_two, from_four,
    base,
    dest_s, failed_s, dest_v, lost_counts, lost_sources,
    block_v, rows_v, extra_v, info_v, small_sem, block_sem, move_sem,
):
    lost_rows = fails * cap
    slots, width = base.shape[0], rows_v.shape[1]
    rows = block_v.shape[0] // fails
    half, eighth = width // 2, width // 8
    group = lax.axis_index("pipe")
    me = lax.axis_index("dp")
    small = [
        pltpu.make_async_copy(failed, failed_s, small_sem.at[0]),
        pltpu.make_async_copy(dest, dest_s, small_sem.at[1]),
        pltpu.make_async_copy(dest, dest_v, small_sem.at[2]),
    ]
    for copy in small:
        copy.start()
    for copy in small:
        copy.wait()
    blocks = [
        pltpu.make_async_copy(
            replica.at[pl.ds(pl.multiple_of(failed_s[i, group] * rows, rows), rows), :],
            block_v.at[pl.ds(i * rows, rows), :],
            block_sem.at[i],
        )
        for i in range(fails)
    ]
    for copy in blocks:
        copy.start()

    every = ranks * rows
    row_ids = lax.broadcasted_iota(jnp.int32, (every, every), 0)
    column_ids = lax.broadcasted_iota(jnp.int32, (every, every), 1)
    place = dest_v[pl.ds(group, 1), :]
    mine = jnp.where(lax.div(place, rows) == me, 1.0, 0.0)
    mine_down = jnp.sum(jnp.where(row_ids == column_ids, mine, 0.0), axis=1, keepdims=True)
    earlier = (row_ids < column_ids) & (lax.div(row_ids, rows) == lax.div(column_ids, rows))
    order = jnp.sum(jnp.where(earlier, mine_down, 0.0), axis=0, keepdims=True).astype(jnp.int32)
    columns = lax.broadcasted_iota(jnp.int32, (1, every), 1)
    slot_of = jnp.where(mine > 0.5, (lax.div(columns, rows) ^ me) * cap + order, -1)
    slot_rows = lax.broadcasted_iota(jnp.int32, (slots, every), 0)
    found = slot_rows == slot_of
    place_in = lax.rem(place, rows).astype(jnp.float32)
    places = jnp.sum(jnp.where(found, place_in + 1.0, 0.0), axis=1, keepdims=True) - 1.0
    slot_ids = lax.broadcasted_iota(jnp.int32, (slots, 128), 0)
    source = lax.div(slot_ids, cap) ^ me
    is_lost = source == failed_s[0, group]
    for i in range(1, fails):
        is_lost = is_lost | (source == failed_s[i, group])
    lanes = lax.broadcasted_iota(jnp.int32, (slots, 128), 1)
    info_v[...] = jnp.where(lanes == PLACE_LANE, places, jnp.where(is_lost, 1.0, 0.0))
    send_info = pltpu.make_async_copy(info_v, base.at[:, pl.ds(width, 128)], small_sem.at[0])
    send_info.start()
    for j in range(lost_rows):
        lost_sources[j] = 0
    for i in range(fails):
        lost_counts[i] = 0
        for r in range(rows):

            @pl.when(lax.div(dest_s[group, failed_s[i, group] * rows + r], rows) == me)
            def _(i=i, r=r):
                order = lost_counts[i]
                lost_sources[i * cap + order] = i * rows + r
                lost_counts[i] = order + 1

    is_failed = failed_s[0, group] == me
    sibling_failed = failed_s[0, group] == (me ^ 1)
    for i in range(1, fails):
        is_failed = is_failed | (failed_s[i, group] == me)
        sibling_failed = sibling_failed | (failed_s[i, group] == (me ^ 1))
    for copy in blocks:
        copy.wait()

    @pl.when(jnp.logical_not(is_failed))
    def _():
        rows_v[...] = block_v[...].astype(jnp.float32)

    @pl.when(is_failed)
    def _():
        def take(source, i, first, columns):
            return pltpu.make_async_copy(
                source.at[i, :, pl.ds(width, columns)], extra_v.at[pl.ds(i * cap, cap), pl.ds(first, columns)], move_sem
            )

        @pl.when(jnp.logical_not(sibling_failed))
        def _():
            copies = [take(from_one, i, 0, half) for i in range(fails)]
            for copy in copies:
                copy.start()
            for copy in copies:
                copy.wait()

        @pl.when(sibling_failed)
        def _():
            parts = (from_two.at[0], from_two.at[1], from_four.at[0], from_four.at[1])
            copies = [take(ref, i, n * eighth, eighth) for i in range(fails) for n, ref in enumerate(parts)]
            for copy in copies:
                copy.start()
            for copy in copies:
                copy.wait()

        packed = extra_v[...]
        rows_v[0:lost_rows, 0:half] = decode_short(signed_high(packed))
        rows_v[0:lost_rows, half:width] = decode_short(signed_low(packed))
        for j in range(lost_rows):
            lost_sources[j] = j

    moves = [
        pltpu.make_async_copy(
            rows_v.at[pl.ds(lost_sources[i * cap + order], 1), :],
            base.at[pl.ds((failed_s[i, group] ^ me) * cap + order, 1), pl.ds(0, width)],
            move_sem,
        )
        for i in range(fails)
        for order in range(cap)
    ]
    for copy in moves:
        copy.start()
    for copy in moves:
        copy.wait()
    send_info.wait()


def update_kernel(
    ranks, cap, elements,
    sums, base, *refs,
):
    kinds = sent_kinds(ranks)
    arrived = dict(zip(kinds, refs))
    for k, ref in zip(range(2, ranks, 2), refs[len(kinds):ranks]):
        arrived[k], arrived[k + 1] = arrived[k].at[0], ref.at[1]
    (new_master, new_first, new_second, info_s, sums_v, words, base_v,
     master_o, first_o, second_o, small_sem, word_sem, out_sem) = refs[ranks:]
    rows, width = new_master.shape
    slots = base_v.shape[0]
    chunk = width // UPDATE_CHUNKS
    info = pl.ds(width, 128)
    small = [
        pltpu.make_async_copy(source, target, small_sem.at[i])
        for i, (source, target) in enumerate(
            ((sums, sums_v), (base.at[:, info], base_v.at[:, info]), (base.at[:, info], info_s))
        )
    ]
    for copy in small:
        copy.start()
    for part in range(UPDATE_CHUNKS):
        columns = pl.ds(part * chunk, chunk)
        copies = [pltpu.make_async_copy(base.at[:, columns], base_v.at[:, columns], word_sem.at[part])] + [
            pltpu.make_async_copy(
                arrived[k].at[:, :, columns], words.at[:, pl.ds(k * cap, cap), columns], word_sem.at[part]
            )
            for k in range(ranks)
        ]
        for copy in copies:
            copy.start()
    for copy in small:
        copy.wait()

    grad_total = jnp.sum(jnp.sum(sums_v[...], axis=0, keepdims=True), axis=1, keepdims=True)
    clip_scale = jnp.minimum(1.0, 1.0 / jnp.sqrt(grad_total / elements + clip_eps))
    is_lost = base_v[:, width + LOST_LANE:width + LOST_LANE + 1] > 0.5
    keep_one = jnp.where(is_lost, 0.0, beta_one)
    keep_two = jnp.where(is_lost, 0.0, beta_two)
    scale_one = 1.0 / (1.0 - beta_one**STEP)
    scale_two = 1.0 / (1.0 - beta_two**STEP)

    for part in range(UPDATE_CHUNKS):
        columns = pl.ds(part * chunk, chunk)
        for ref in (words.at[:, :, columns], base_v.at[:, columns]):
            pltpu.make_async_copy(ref, ref, word_sem.at[part]).wait()
        one, two = words[0, :, columns], words[1, :, columns]
        weights = jnp.where(is_lost, base_v[:, columns], decode_log(signed_high(one), MASTER_MAX))
        first = decode_log(signed_low(one), FIRST_MAX)
        second = decode_second(lax.shift_right_logical(two, 16))
        grads = decode_short(signed_low(two)) * clip_scale
        first_new = keep_one * first + (1.0 - beta_one) * grads
        second_new = keep_two * second + (1.0 - beta_two) * grads * grads
        spread = second_new * scale_two
        root = spread * lax.rsqrt(jnp.maximum(spread, 1e-37))
        step = first_new * (learn_rate * scale_one) / (root + adam_eps)
        master_o[:, columns] = weights * (1.0 - learn_rate * decay_rate) - step
        first_o[:, columns] = first_new
        second_o[:, columns] = second_new
        for slot in range(slots):
            place = info_s[slot, PLACE_LANE].astype(jnp.int32)

            def move(slot=slot, place=place, columns=columns):
                return [
                    pltpu.make_async_copy(a.at[pl.ds(slot, 1), columns], b.at[pl.ds(place, 1), columns], out_sem)
                    for a, b in ((master_o, new_master), (first_o, new_first), (second_o, new_second))
                ]

            if slots == rows:
                for copy in move():
                    copy.start()
            else:

                @pl.when(place >= 0)
                def _(move=move):
                    for copy in move():
                        copy.start()

    for ref in (new_master, new_first, new_second):
        pltpu.make_async_copy(ref, ref, out_sem).wait()


def local(master, moment1, moment2, quant_grad, grad_exponent, replica_params, failed, dest):
    ranks = lax.axis_size("dp")
    devices = ranks * lax.axis_size("pipe")
    _, rows, width = master.shape
    failed = failed.T
    fails = failed.shape[0]
    assert fails == 2 and ranks >= 8 and ranks & (ranks - 1) == 0
    cap = (rows + ranks - 1) // ranks
    slots = ranks * cap
    kinds = sent_kinds(ranks)
    lost_rows = fails * cap
    i32, f32 = jnp.int32, jnp.float32
    vmem, smem, dma = pltpu.VMEM, pltpu.SMEM, pltpu.SemaphoreType.DMA

    packed = pl.pallas_call(
        functools.partial(pack_kernel, ranks, cap, fails, devices),
        out_shape=[jax.ShapeDtypeStruct(payload_shape(k, cap, width), i32) for k in kinds]
        + [jax.ShapeDtypeStruct((devices, 128), f32)],
        in_specs=[ANY] * 8,
        out_specs=[ANY] * (len(kinds) + 1),
        scratch_shapes=[
            smem(dest.shape, i32), smem(failed.shape, i32), smem((1, rows), i32),
            smem((ranks,), i32), smem((slots,), i32),
            smem((ranks * fails,), i32), smem((ranks * lost_rows,), i32),
            vmem((rows, width), f32), vmem((rows, width), f32), vmem((rows, width), f32),
            vmem((rows, width), jnp.bfloat16),
            vmem((fails * rows, width), jnp.bfloat16), vmem((fails * rows, width), f32),
            vmem((lost_rows, width), f32),
            vmem((2, rows, width), i32),
            vmem((lost_rows, width // 2), i32), vmem((devices, 128), f32),
            dma((3,)), dma((PACK_CHUNKS, 4)), dma((fails,)), dma, dma,
        ],
        compiler_params=pltpu.CompilerParams(vmem_limit_bytes=PACK_VMEM),
        name="pack",
    )(dest, failed, grad_exponent, master[0], moment1[0], moment2[0], quant_grad[0], replica_params[0, 0])
    payloads, total = dict(zip(kinds, packed)), packed[-1]

    def send(k, value):
        return lax.ppermute(value, "dp", [(i, i ^ k) for i in range(ranks)])

    arrived = {0: payloads[0], 1: send(1, payloads[1])}
    for k in range(2, ranks, 2):
        value = payloads[k]
        if k not in (2, 4):
            value, _ = lax.optimization_barrier((value, arrived[1]))
        arrived[k] = send(k, value)
    sums = lax.all_to_all(total, ("pipe", "dp"), split_axis=0, concat_axis=0, tiled=True)
    handed = []
    for k in range(2, ranks, 2):
        value, _ = lax.optimization_barrier((arrived[k], sums))
        handed.append(send(1, value))

    base = pl.pallas_call(
        functools.partial(base_kernel, ranks, cap, fails),
        out_shape=jax.ShapeDtypeStruct((slots, width + 128), f32),
        in_specs=[ANY] * 6,
        out_specs=ANY,
        scratch_shapes=[
            smem(dest.shape, i32), smem(failed.shape, i32), vmem(dest.shape, i32),
            smem((fails,), i32), smem((lost_rows,), i32),
            vmem((fails * rows, width), jnp.bfloat16), vmem((fails * rows, width), f32),
            vmem((lost_rows, width // 2), i32), vmem((slots, 128), f32),
            dma((3,)), dma((fails,)), dma,
        ],
        compiler_params=pltpu.CompilerParams(vmem_limit_bytes=OTHER_VMEM),
        name="base",
    )(dest, failed, replica_params[0, 0], arrived[1], arrived[2], arrived[4])

    outs = pl.pallas_call(
        functools.partial(update_kernel, ranks, cap, devices * rows * width),
        out_shape=[jax.ShapeDtypeStruct((rows, width), f32)] * 3,
        in_specs=[ANY] * (2 + ranks),
        out_specs=[ANY] * 3,
        scratch_shapes=[
            smem((slots, 128), f32), vmem((devices, 128), f32),
            vmem((2, slots, width), i32), vmem((slots, width + 128), f32),
            vmem((slots, width), f32), vmem((slots, width), f32), vmem((slots, width), f32),
            dma((3,)), dma((UPDATE_CHUNKS,)), dma,
        ],
        compiler_params=pltpu.CompilerParams(vmem_limit_bytes=OTHER_VMEM),
        name="update",
    )(sums, base, *[arrived[k] for k in kinds], *handed)
    return tuple(out[None] for out in outs)


def solution(mesh):
    rows3 = P("pipe", "dp", None)
    in_specs = (rows3, rows3, rows3, rows3, P("pipe", "dp"), P("pipe", "dp", None, None), P(), P())
    return jax.shard_map(local, mesh=mesh, in_specs=in_specs, out_specs=(rows3,) * 3, check_vma=False)
```

```python
import functools

import jax
import jax.numpy as jnp
import numpy as np
from jax import lax
from jax.experimental import pallas as pl
from jax.experimental.pallas import tpu as pltpu
from jax.sharding import PartitionSpec as P

STEP = 20

beta_one = 0.9
beta_two = 0.95
learn_rate = 0.00015
decay_rate = 0.1
adam_eps = 1e-08
clip_eps = 1e-06

MASTER_MAX = 0.1201
FIRST_MAX = 3.003
SECOND_MIN = 0.249
SECOND_MAX = 4.501

OCTAVES = 16
LOG_TOP = float(np.log(1.0 + 2.0**OCTAVES))
LOG_STEPS = 32767.0
LN_TWO = float(np.log(2.0))
SECOND_STEPS = 65535.0

PLACE_LANE, LOST_LANE = 0, 1
PACK_PARTS = (5, 3)
EXTRA_AT = 1
UPDATE_PARTS = (3, 5)
PACK_VMEM = 56 * 1024 * 1024
OTHER_VMEM = 12 * 1024 * 1024
ANY = pl.BlockSpec(memory_space=pl.ANY)


def spans(width, parts):
    ends = np.cumsum(parts) * width // sum(parts)
    return [pl.ds(int(end) - part * width // sum(parts), part * width // sum(parts)) for part, end in zip(parts, ends)]


def with_sign(code, x):
    return jnp.where(x < 0, -code, code)


def encode_log(x, top):
    steps = jnp.log(jnp.abs(x) * (2.0**OCTAVES / top) + 1.0) * (LOG_STEPS / LOG_TOP) + 0.5
    return with_sign(steps.astype(jnp.int32), x)


def decode_log(code, top):
    size = jnp.exp2(jnp.abs(code).astype(jnp.float32) * (LOG_TOP / LOG_STEPS / LN_TWO)) * (top / 2.0**OCTAVES) - top / 2.0**OCTAVES
    return with_sign(size, code)


def encode_second(x):
    step = SECOND_STEPS / (SECOND_MAX - SECOND_MIN)
    return (x * step + (0.5 - SECOND_MIN * step)).astype(jnp.int32)


def decode_second(code):
    return code.astype(jnp.float32) * ((SECOND_MAX - SECOND_MIN) / SECOND_STEPS) + SECOND_MIN


def encode_short(x, large=False):
    size = jnp.maximum(jnp.abs(x), 2.0**-126)
    exponent = jnp.floor(jnp.log(size) * (1.0 / LN_TWO) + 0.002)
    if large:
        half = jnp.floor(exponent * 0.5)
        mantissa = size * jnp.exp2(-half) * jnp.exp2(half - exponent)
    else:
        mantissa = size * jnp.exp2(-exponent)
    code = (exponent + mantissa) * 128.0 + (126.0 * 128.0 + 0.5)
    return with_sign(code.astype(jnp.int32), x)


def decode_short(code):
    size = jnp.abs(code)
    exponent = (lax.shift_right_logical(size, 7) - 127).astype(jnp.float32)
    mantissa = (size & 127).astype(jnp.float32) * (1.0 / 128.0) + 1.0
    return with_sign(mantissa * jnp.exp2(exponent), code)


def join(high, low):
    return (high << 16) | (low & 0xFFFF)


def signed_high(word):
    return word >> 16


def signed_low(word):
    return (word << 16) >> 16


def payload_shape(k, cap, width):
    if k < 2:
        return (2, cap, width + k * (width // 2))
    return (2, 2, cap, width + (width // 8 if k in (2, 4) else 0))


def sent_kinds(ranks):
    return [0, 1] + list(range(2, ranks, 2))


def pack_kernel(
    ranks, cap, fails, devices,
    dest, failed, grad_exponent, master, moment1, moment2, quant_grad, replica,
    *refs,
):
    kinds = sent_kinds(ranks)
    payloads, total = dict(zip(kinds, refs)), refs[len(kinds)]
    (dest_s, failed_s, exponent_s, counts, table, lost_counts, lost_table,
     master_v, first_v, second_v, grad_v, block_v, lost_v, picked_v, words, extra_v, total_v,
     small_sem, in_sem, block_sem, pick_sem, out_sem) = refs[len(kinds) + 1:]
    rows, width = master_v.shape
    half, quarter, eighth = width // 2, width // 4, width // 8
    lost_rows = fails * cap
    group = lax.axis_index("pipe")
    me = lax.axis_index("dp")

    small = [
        pltpu.make_async_copy(grad_exponent, exponent_s, small_sem.at[1]),
        pltpu.make_async_copy(failed, failed_s, small_sem.at[0]),
        pltpu.make_async_copy(dest, dest_s, small_sem.at[2]),
    ]
    for copy in small:
        copy.start()
    loads = []
    for part, columns in enumerate(spans(width, PACK_PARTS)):
        copies = [
            pltpu.make_async_copy(source.at[:, columns], target.at[:, columns], in_sem.at[part, i])
            for i, (source, target) in enumerate(
                [(quant_grad, grad_v), (master, master_v), (moment1, first_v), (moment2, second_v)]
            )
        ]
        for copy in copies:
            copy.start()
        loads.append(copies)
    for copy in small:
        copy.wait()
    blocks = [
        pltpu.make_async_copy(
            replica.at[pl.ds(pl.multiple_of(failed_s[i, group] * rows, rows), rows), :],
            block_v.at[pl.ds(i * rows, rows), :],
            block_sem.at[i],
        )
        for i in range(fails)
    ]
    for copy in blocks:
        copy.start()

    for i in range(ranks * cap):
        table[i] = 0
    for i in range(ranks):
        counts[i] = 0
    for r in range(rows):
        target = lax.div(dest_s[group, me * rows + r], rows)
        order = counts[target]
        table[target * cap + order] = r
        counts[target] = order + 1
    for i in range(ranks * lost_rows):
        lost_table[i] = 0
    for i in range(ranks * fails):
        lost_counts[i] = 0
    for i in range(fails):
        for r in range(rows):
            target = lax.div(dest_s[group, failed_s[i, group] * rows + r], rows)
            slot = target * fails + i
            order = lost_counts[slot]
            lost_table[slot * cap + order] = i * rows + r
            lost_counts[slot] = order + 1

    def has_failed(rank):
        found = failed_s[0, group] == rank
        for i in range(1, fails):
            found = found | (failed_s[i, group] == rank)
        return found

    helped = jnp.where(has_failed(me ^ 1), me ^ 1, jnp.where(has_failed(me ^ 2) & has_failed(me ^ 3), me ^ 2, me ^ 4))

    row_ids = lax.broadcasted_iota(jnp.int32, (rows, 128), 0)
    exponents = jnp.zeros((rows, 128), jnp.float32)
    for r in range(rows):
        exponents = jnp.where(row_ids == r, exponent_s[0, r].astype(jnp.float32), exponents)
    row_scale = jnp.exp2(exponents)[:, :1]

    sums = jnp.zeros((8, 128), jnp.float32)
    picks = []
    for part, columns in enumerate(spans(width, PACK_PARTS)):
        if part == EXTRA_AT:
            for copy in blocks:
                copy.wait()
            lost_v[...] = block_v[...].astype(jnp.float32)
            for j in range(lost_rows):
                source = lost_table[helped * lost_rows + j]
                picks.append(pltpu.make_async_copy(lost_v.at[pl.ds(source, 1), :], picked_v.at[pl.ds(j, 1), :], pick_sem))
            for copy in picks:
                copy.start()
        for copy in loads[part]:
            copy.wait()
        grad = grad_v[:, columns].astype(jnp.float32) * row_scale
        sums += jnp.sum((grad * grad).reshape(rows // 8, 8, -1, 128), axis=(0, 2))
        words[0, :, columns] = join(encode_log(master_v[:, columns], MASTER_MAX), encode_log(first_v[:, columns], FIRST_MAX))
        words[1, :, columns] = join(encode_second(second_v[:, columns]), encode_short(grad))
        for k in reversed(range(ranks)):
            for order in range(cap):
                row = table[(me ^ k) * cap + order]
                target = payloads[k] if k < 2 else payloads[k - k % 2].at[k % 2]
                copy = pltpu.make_async_copy(
                    words.at[:, pl.ds(row, 1), columns], target.at[:, pl.ds(order, 1), columns], out_sem
                )
                copy.start()
    total_v[...] = jnp.broadcast_to(jnp.sum(sums, axis=0, keepdims=True), (devices, 128))
    pltpu.make_async_copy(total_v, total, out_sem).start()

    for copy in picks:
        copy.wait()
    extra_v[...] = join(encode_short(picked_v[:, :half], True), encode_short(picked_v[:, half:], True))
    extras = [(payloads[1], 0, half)] + [
        (payloads[k].at[part], first + part * eighth, eighth)
        for k, first in ((2, 0), (4, quarter))
        for part in range(2)
    ]
    for target, first_column, columns in extras:
        for i in range(fails):
            copy = pltpu.make_async_copy(
                extra_v.at[pl.ds(i * cap, cap), pl.ds(first_column, columns)],
                target.at[i, :, pl.ds(width, columns)],
                out_sem,
            )
            copy.start()
    for ref in refs[:len(kinds) + 1]:
        pltpu.make_async_copy(ref, ref, out_sem).wait()


def base_kernel(
    ranks, cap, fails,
    dest, failed, replica, from_one, from_two, from_four,
    base,
    dest_s, failed_s, dest_v, lost_counts, lost_sources,
    block_v, rows_v, extra_v, info_v, small_sem, block_sem, move_sem,
):
    lost_rows = fails * cap
    slots, width = base.shape[0], rows_v.shape[1]
    rows = block_v.shape[0] // fails
    half, eighth = width // 2, width // 8
    group = lax.axis_index("pipe")
    me = lax.axis_index("dp")
    small = [
        pltpu.make_async_copy(failed, failed_s, small_sem.at[0]),
        pltpu.make_async_copy(dest, dest_s, small_sem.at[1]),
        pltpu.make_async_copy(dest, dest_v, small_sem.at[2]),
    ]
    for copy in small:
        copy.start()
    for copy in small:
        copy.wait()
    blocks = [
        pltpu.make_async_copy(
            replica.at[pl.ds(pl.multiple_of(failed_s[i, group] * rows, rows), rows), :],
            block_v.at[pl.ds(i * rows, rows), :],
            block_sem.at[i],
        )
        for i in range(fails)
    ]
    for copy in blocks:
        copy.start()

    every = ranks * rows
    row_ids = lax.broadcasted_iota(jnp.int32, (every, every), 0)
    column_ids = lax.broadcasted_iota(jnp.int32, (every, every), 1)
    place = dest_v[pl.ds(group, 1), :]
    mine = jnp.where(lax.div(place, rows) == me, 1.0, 0.0)
    mine_down = jnp.sum(jnp.where(row_ids == column_ids, mine, 0.0), axis=1, keepdims=True)
    earlier = (row_ids < column_ids) & (lax.div(row_ids, rows) == lax.div(column_ids, rows))
    order = jnp.sum(jnp.where(earlier, mine_down, 0.0), axis=0, keepdims=True).astype(jnp.int32)
    columns = lax.broadcasted_iota(jnp.int32, (1, every), 1)
    slot_of = jnp.where(mine > 0.5, (lax.div(columns, rows) ^ me) * cap + order, -1)
    slot_rows = lax.broadcasted_iota(jnp.int32, (slots, every), 0)
    found = slot_rows == slot_of
    place_in = lax.rem(place, rows).astype(jnp.float32)
    places = jnp.sum(jnp.where(found, place_in + 1.0, 0.0), axis=1, keepdims=True) - 1.0
    slot_ids = lax.broadcasted_iota(jnp.int32, (slots, 128), 0)
    source = lax.div(slot_ids, cap) ^ me
    is_lost = source == failed_s[0, group]
    for i in range(1, fails):
        is_lost = is_lost | (source == failed_s[i, group])
    lanes = lax.broadcasted_iota(jnp.int32, (slots, 128), 1)
    info_v[...] = jnp.where(lanes == PLACE_LANE, places, jnp.where(is_lost, 1.0, 0.0))
    send_info = pltpu.make_async_copy(info_v, base.at[:, pl.ds(width, 128)], small_sem.at[0])
    send_info.start()
    for j in range(lost_rows):
        lost_sources[j] = 0
    for i in range(fails):
        lost_counts[i] = 0
        for r in range(rows):

            @pl.when(lax.div(dest_s[group, failed_s[i, group] * rows + r], rows) == me)
            def _(i=i, r=r):
                order = lost_counts[i]
                lost_sources[i * cap + order] = i * rows + r
                lost_counts[i] = order + 1

    is_failed = failed_s[0, group] == me
    sibling_failed = failed_s[0, group] == (me ^ 1)
    for i in range(1, fails):
        is_failed = is_failed | (failed_s[i, group] == me)
        sibling_failed = sibling_failed | (failed_s[i, group] == (me ^ 1))
    for copy in blocks:
        copy.wait()

    @pl.when(jnp.logical_not(is_failed))
    def _():
        rows_v[...] = block_v[...].astype(jnp.float32)

    @pl.when(is_failed)
    def _():
        def take(source, i, first, columns):
            return pltpu.make_async_copy(
                source.at[i, :, pl.ds(width, columns)], extra_v.at[pl.ds(i * cap, cap), pl.ds(first, columns)], move_sem
            )

        @pl.when(jnp.logical_not(sibling_failed))
        def _():
            copies = [take(from_one, i, 0, half) for i in range(fails)]
            for copy in copies:
                copy.start()
            for copy in copies:
                copy.wait()

        @pl.when(sibling_failed)
        def _():
            parts = (from_two.at[0], from_two.at[1], from_four.at[0], from_four.at[1])
            copies = [take(ref, i, n * eighth, eighth) for i in range(fails) for n, ref in enumerate(parts)]
            for copy in copies:
                copy.start()
            for copy in copies:
                copy.wait()

        packed = extra_v[...]
        rows_v[0:lost_rows, 0:half] = decode_short(signed_high(packed))
        rows_v[0:lost_rows, half:width] = decode_short(signed_low(packed))
        for j in range(lost_rows):
            lost_sources[j] = j

    moves = [
        pltpu.make_async_copy(
            rows_v.at[pl.ds(lost_sources[i * cap + order], 1), :],
            base.at[pl.ds((failed_s[i, group] ^ me) * cap + order, 1), pl.ds(0, width)],
            move_sem,
        )
        for i in range(fails)
        for order in range(cap)
    ]
    for copy in moves:
        copy.start()
    for copy in moves:
        copy.wait()
    send_info.wait()


def update_kernel(
    ranks, cap, elements,
    sums, base, *refs,
):
    kinds = sent_kinds(ranks)
    arrived = dict(zip(kinds, refs))
    for k, ref in zip(range(2, ranks, 2), refs[len(kinds):ranks]):
        arrived[k], arrived[k + 1] = arrived[k].at[0], ref.at[1]
    (new_master, new_first, new_second, info_s, sums_v, words, base_v,
     master_o, first_o, second_o, small_sem, word_sem, out_sem) = refs[ranks:]
    rows, width = new_master.shape
    slots = base_v.shape[0]
    info = pl.ds(width, 128)
    small = [
        pltpu.make_async_copy(source, target, small_sem.at[i])
        for i, (source, target) in enumerate(
            ((sums, sums_v), (base.at[:, info], base_v.at[:, info]), (base.at[:, info], info_s))
        )
    ]
    for copy in small:
        copy.start()
    for part, columns in enumerate(spans(width, UPDATE_PARTS)):
        copies = [pltpu.make_async_copy(base.at[:, columns], base_v.at[:, columns], word_sem.at[part])] + [
            pltpu.make_async_copy(
                arrived[k].at[:, :, columns], words.at[:, pl.ds(k * cap, cap), columns], word_sem.at[part]
            )
            for k in range(ranks)
        ]
        for copy in copies:
            copy.start()
    for copy in small:
        copy.wait()

    grad_total = jnp.sum(jnp.sum(sums_v[...], axis=0, keepdims=True), axis=1, keepdims=True)
    clip_scale = jnp.minimum(1.0, 1.0 / jnp.sqrt(grad_total / elements + clip_eps))
    is_lost = base_v[:, width + LOST_LANE:width + LOST_LANE + 1] > 0.5
    keep_one = jnp.where(is_lost, 0.0, beta_one)
    keep_two = jnp.where(is_lost, 0.0, beta_two)
    scale_one = 1.0 / (1.0 - beta_one**STEP)
    scale_two = 1.0 / (1.0 - beta_two**STEP)

    for part, columns in enumerate(spans(width, UPDATE_PARTS)):
        for ref in (words.at[:, :, columns], base_v.at[:, columns]):
            pltpu.make_async_copy(ref, ref, word_sem.at[part]).wait()
        one, two = words[0, :, columns], words[1, :, columns]
        weights = jnp.where(is_lost, base_v[:, columns], decode_log(signed_high(one), MASTER_MAX))
        first = decode_log(signed_low(one), FIRST_MAX)
        second = decode_second(lax.shift_right_logical(two, 16))
        grads = decode_short(signed_low(two)) * clip_scale
        first_new = keep_one * first + (1.0 - beta_one) * grads
        second_new = keep_two * second + (1.0 - beta_two) * grads * grads
        spread = second_new * scale_two
        root = spread * lax.rsqrt(jnp.maximum(spread, 1e-37))
        step = first_new * (learn_rate * scale_one) / (root + adam_eps)
        master_o[:, columns] = weights * (1.0 - learn_rate * decay_rate) - step
        first_o[:, columns] = first_new
        second_o[:, columns] = second_new
        for slot in range(slots):
            place = info_s[slot, PLACE_LANE].astype(jnp.int32)

            def move(slot=slot, place=place, columns=columns):
                return [
                    pltpu.make_async_copy(a.at[pl.ds(slot, 1), columns], b.at[pl.ds(place, 1), columns], out_sem)
                    for a, b in ((master_o, new_master), (first_o, new_first), (second_o, new_second))
                ]

            if slots == rows:
                for copy in move():
                    copy.start()
            else:

                @pl.when(place >= 0)
                def _(move=move):
                    for copy in move():
                        copy.start()

    for ref in (new_master, new_first, new_second):
        pltpu.make_async_copy(ref, ref, out_sem).wait()


def local(master, moment1, moment2, quant_grad, grad_exponent, replica_params, failed, dest):
    ranks = lax.axis_size("dp")
    devices = ranks * lax.axis_size("pipe")
    _, rows, width = master.shape
    failed = failed.T
    fails = failed.shape[0]
    assert fails == 2 and ranks >= 8 and ranks & (ranks - 1) == 0
    cap = (rows + ranks - 1) // ranks
    slots = ranks * cap
    kinds = sent_kinds(ranks)
    lost_rows = fails * cap
    i32, f32 = jnp.int32, jnp.float32
    vmem, smem, dma = pltpu.VMEM, pltpu.SMEM, pltpu.SemaphoreType.DMA

    packed = pl.pallas_call(
        functools.partial(pack_kernel, ranks, cap, fails, devices),
        out_shape=[jax.ShapeDtypeStruct(payload_shape(k, cap, width), i32) for k in kinds]
        + [jax.ShapeDtypeStruct((devices, 128), f32)],
        in_specs=[ANY] * 8,
        out_specs=[ANY] * (len(kinds) + 1),
        scratch_shapes=[
            smem(dest.shape, i32), smem(failed.shape, i32), smem((1, rows), i32),
            smem((ranks,), i32), smem((slots,), i32),
            smem((ranks * fails,), i32), smem((ranks * lost_rows,), i32),
            vmem((rows, width), f32), vmem((rows, width), f32), vmem((rows, width), f32),
            vmem((rows, width), jnp.bfloat16),
            vmem((fails * rows, width), jnp.bfloat16), vmem((fails * rows, width), f32),
            vmem((lost_rows, width), f32),
            vmem((2, rows, width), i32),
            vmem((lost_rows, width // 2), i32), vmem((devices, 128), f32),
            dma((3,)), dma((len(PACK_PARTS), 4)), dma((fails,)), dma, dma,
        ],
        compiler_params=pltpu.CompilerParams(vmem_limit_bytes=PACK_VMEM),
        name="pack",
    )(dest, failed, grad_exponent, master[0], moment1[0], moment2[0], quant_grad[0], replica_params[0, 0])
    payloads, total = dict(zip(kinds, packed)), packed[-1]

    def send(k, value):
        return lax.ppermute(value, "dp", [(i, i ^ k) for i in range(ranks)])

    arrived = {0: payloads[0], 1: send(1, payloads[1])}
    for k in range(2, ranks, 2):
        value = payloads[k]
        if k not in (2, 4):
            value, _ = lax.optimization_barrier((value, arrived[1]))
        arrived[k] = send(k, value)
    sums = lax.all_to_all(total, ("pipe", "dp"), split_axis=0, concat_axis=0, tiled=True)
    handed = []
    for k in range(2, ranks, 2):
        value, _ = lax.optimization_barrier((arrived[k], sums))
        handed.append(send(1, value))

    base = pl.pallas_call(
        functools.partial(base_kernel, ranks, cap, fails),
        out_shape=jax.ShapeDtypeStruct((slots, width + 128), f32),
        in_specs=[ANY] * 6,
        out_specs=ANY,
        scratch_shapes=[
            smem(dest.shape, i32), smem(failed.shape, i32), vmem(dest.shape, i32),
            smem((fails,), i32), smem((lost_rows,), i32),
            vmem((fails * rows, width), jnp.bfloat16), vmem((fails * rows, width), f32),
            vmem((lost_rows, width // 2), i32), vmem((slots, 128), f32),
            dma((3,)), dma((fails,)), dma,
        ],
        compiler_params=pltpu.CompilerParams(vmem_limit_bytes=OTHER_VMEM),
        name="base",
    )(dest, failed, replica_params[0, 0], arrived[1], arrived[2], arrived[4])

    outs = pl.pallas_call(
        functools.partial(update_kernel, ranks, cap, devices * rows * width),
        out_shape=[jax.ShapeDtypeStruct((rows, width), f32)] * 3,
        in_specs=[ANY] * (2 + ranks),
        out_specs=[ANY] * 3,
        scratch_shapes=[
            smem((slots, 128), f32), vmem((devices, 128), f32),
            vmem((2, slots, width), i32), vmem((slots, width + 128), f32),
            vmem((slots, width), f32), vmem((slots, width), f32), vmem((slots, width), f32),
            dma((3,)), dma((len(UPDATE_PARTS),)), dma,
        ],
        compiler_params=pltpu.CompilerParams(vmem_limit_bytes=OTHER_VMEM),
        name="update",
    )(sums, base, *[arrived[k] for k in kinds], *handed)
    return tuple(out[None] for out in outs)


def solution(mesh):
    rows3 = P("pipe", "dp", None)
    in_specs = (rows3, rows3, rows3, rows3, P("pipe", "dp"), P("pipe", "dp", None, None), P(), P())
    return jax.shard_map(local, mesh=mesh, in_specs=in_specs, out_specs=(rows3,) * 3, check_vma=False)
```

```python
import functools

import jax
import jax.numpy as jnp
import numpy as np
from jax import lax
from jax.experimental import pallas as pl
from jax.experimental.pallas import tpu as pltpu
from jax.sharding import PartitionSpec as P

STEP = 20

beta_one = 0.9
beta_two = 0.95
learn_rate = 0.00015
decay_rate = 0.1
adam_eps = 1e-08
clip_eps = 1e-06

MASTER_MAX = 0.1201
FIRST_MAX = 3.003
SECOND_MIN = 0.249
SECOND_MAX = 4.501

OCTAVES = 16
LOG_TOP = float(np.log(1.0 + 2.0**OCTAVES))
LOG_STEPS = 32767.0
LN_TWO = float(np.log(2.0))
SECOND_STEPS = 65535.0

PLACE_LANE, LOST_LANE = 0, 1
PACK_PARTS = (5, 3)
EXTRA_AT = 1
UPDATE_PARTS = (3, 5)
PACK_VMEM = 56 * 1024 * 1024
OTHER_VMEM = 12 * 1024 * 1024
ANY = pl.BlockSpec(memory_space=pl.ANY)


def spans(width, parts):
    ends = np.cumsum(parts) * width // sum(parts)
    return [pl.ds(int(end) - part * width // sum(parts), part * width // sum(parts)) for part, end in zip(parts, ends)]


def with_sign(code, x):
    return jnp.where(x < 0, -code, code)


def encode_log(x, top):
    steps = jnp.log(jnp.abs(x) * (2.0**OCTAVES / top) + 1.0) * (LOG_STEPS / LOG_TOP) + 0.5
    return with_sign(steps.astype(jnp.int32), x)


def decode_log(code, top):
    size = jnp.exp2(jnp.abs(code).astype(jnp.float32) * (LOG_TOP / LOG_STEPS / LN_TWO)) * (top / 2.0**OCTAVES) - top / 2.0**OCTAVES
    return with_sign(size, code)


def encode_second(x):
    step = SECOND_STEPS / (SECOND_MAX - SECOND_MIN)
    return (x * step + (0.5 - SECOND_MIN * step)).astype(jnp.int32)


def decode_second(code):
    return code.astype(jnp.float32) * ((SECOND_MAX - SECOND_MIN) / SECOND_STEPS) + SECOND_MIN


def encode_short(x, large=False):
    size = jnp.maximum(jnp.abs(x), 2.0**-126)
    exponent = jnp.floor(jnp.log(size) * (1.0 / LN_TWO) + 0.002)
    if large:
        half = jnp.floor(exponent * 0.5)
        mantissa = size * jnp.exp2(-half) * jnp.exp2(half - exponent)
    else:
        mantissa = size * jnp.exp2(-exponent)
    code = (exponent + mantissa) * 128.0 + (126.0 * 128.0 + 0.5)
    return with_sign(code.astype(jnp.int32), x)


def decode_short(code):
    size = jnp.abs(code)
    exponent = (lax.shift_right_logical(size, 7) - 127).astype(jnp.float32)
    mantissa = (size & 127).astype(jnp.float32) * (1.0 / 128.0) + 1.0
    return with_sign(mantissa * jnp.exp2(exponent), code)


def join(high, low):
    return (high << 16) | (low & 0xFFFF)


def signed_high(word):
    return word >> 16


def signed_low(word):
    return (word << 16) >> 16


def payload_shape(k, cap, width):
    if k < 2:
        return (2, cap, width + k * (width // 2))
    return (2, 2, cap, width + (width // 8 if k in (2, 4) else 0))


def sent_kinds(ranks):
    return [0, 1] + list(range(2, ranks, 2))


def pack_kernel(
    ranks, cap, fails, devices,
    dest, failed, grad_exponent, master, moment1, moment2, quant_grad, replica,
    *refs,
):
    kinds = sent_kinds(ranks)
    payloads, total = dict(zip(kinds, refs)), refs[len(kinds)]
    (dest_s, failed_s, exponent_s, counts, table, lost_counts, lost_table,
     master_v, first_v, second_v, grad_v, block_v, lost_v, picked_v, words, extra_v, total_v,
     small_sem, in_sem, block_sem, pick_sem, out_sem) = refs[len(kinds) + 1:]
    rows, width = master_v.shape
    half, quarter, eighth = width // 2, width // 4, width // 8
    lost_rows = fails * cap
    group = lax.axis_index("pipe")
    me = lax.axis_index("dp")

    small = [
        pltpu.make_async_copy(grad_exponent, exponent_s, small_sem.at[1]),
        pltpu.make_async_copy(failed, failed_s, small_sem.at[0]),
        pltpu.make_async_copy(dest, dest_s, small_sem.at[2]),
    ]
    for copy in small:
        copy.start()
    loads = []
    for part, columns in enumerate(spans(width, PACK_PARTS)):
        copies = [
            pltpu.make_async_copy(source.at[:, columns], target.at[:, columns], in_sem.at[part, i])
            for i, (source, target) in enumerate(
                [(quant_grad, grad_v), (master, master_v), (moment1, first_v), (moment2, second_v)]
            )
        ]
        for copy in copies:
            copy.start()
        loads.append(copies)
    for copy in small:
        copy.wait()
    blocks = [
        pltpu.make_async_copy(
            replica.at[pl.ds(pl.multiple_of(failed_s[i, group] * rows, rows), rows), :],
            block_v.at[pl.ds(i * rows, rows), :],
            block_sem.at[i],
        )
        for i in range(fails)
    ]
    for copy in blocks:
        copy.start()

    for i in range(ranks * cap):
        table[i] = 0
    for i in range(ranks):
        counts[i] = 0
    for r in range(rows):
        target = lax.div(dest_s[group, me * rows + r], rows)
        order = counts[target]
        table[target * cap + order] = r
        counts[target] = order + 1
    for i in range(ranks * lost_rows):
        lost_table[i] = 0
    for i in range(ranks * fails):
        lost_counts[i] = 0
    for i in range(fails):
        for r in range(rows):
            target = lax.div(dest_s[group, failed_s[i, group] * rows + r], rows)
            slot = target * fails + i
            order = lost_counts[slot]
            lost_table[slot * cap + order] = i * rows + r
            lost_counts[slot] = order + 1

    def has_failed(rank):
        found = failed_s[0, group] == rank
        for i in range(1, fails):
            found = found | (failed_s[i, group] == rank)
        return found

    helped = jnp.where(has_failed(me ^ 1), me ^ 1, jnp.where(has_failed(me ^ 2) & has_failed(me ^ 3), me ^ 2, me ^ 4))

    row_ids = lax.broadcasted_iota(jnp.int32, (rows, 128), 0)
    exponents = jnp.zeros((rows, 128), jnp.float32)
    for r in range(rows):
        exponents = jnp.where(row_ids == r, exponent_s[0, r].astype(jnp.float32), exponents)
    row_scale = jnp.exp2(exponents)[:, :1]

    sums = jnp.zeros((8, 128), jnp.float32)
    picks = []
    for part, columns in enumerate(spans(width, PACK_PARTS)):
        if part == EXTRA_AT:
            for copy in blocks:
                copy.wait()
            lost_v[...] = block_v[...].astype(jnp.float32)
            for j in range(lost_rows):
                source = lost_table[helped * lost_rows + j]
                picks.append(pltpu.make_async_copy(lost_v.at[pl.ds(source, 1), :], picked_v.at[pl.ds(j, 1), :], pick_sem))
            for copy in picks:
                copy.start()
        for copy in loads[part]:
            copy.wait()
        grad = grad_v[:, columns].astype(jnp.float32) * row_scale
        sums += jnp.sum((grad * grad).reshape(rows // 8, 8, -1, 128), axis=(0, 2))
        words[0, :, columns] = join(encode_log(master_v[:, columns], MASTER_MAX), encode_log(first_v[:, columns], FIRST_MAX))
        words[1, :, columns] = join(encode_second(second_v[:, columns]), encode_short(grad))
        for k in reversed(range(ranks)):
            for order in range(cap):
                row = table[(me ^ k) * cap + order]
                target = payloads[k] if k < 2 else payloads[k - k % 2].at[k % 2]
                copy = pltpu.make_async_copy(
                    words.at[:, pl.ds(row, 1), columns], target.at[:, pl.ds(order, 1), columns], out_sem
                )
                copy.start()
    total_v[...] = jnp.broadcast_to(jnp.sum(sums, axis=0, keepdims=True), (devices, 128))
    pltpu.make_async_copy(total_v, total, out_sem).start()

    for copy in picks:
        copy.wait()
    extra_v[...] = join(encode_short(picked_v[:, :half], True), encode_short(picked_v[:, half:], True))
    extras = [(payloads[1], 0, half)] + [
        (payloads[k].at[part], first + part * eighth, eighth)
        for k, first in ((2, 0), (4, quarter))
        for part in range(2)
    ]
    for target, first_column, columns in extras:
        for i in range(fails):
            copy = pltpu.make_async_copy(
                extra_v.at[pl.ds(i * cap, cap), pl.ds(first_column, columns)],
                target.at[i, :, pl.ds(width, columns)],
                out_sem,
            )
            copy.start()
    for ref in refs[:len(kinds) + 1]:
        pltpu.make_async_copy(ref, ref, out_sem).wait()


def base_kernel(
    ranks, cap, fails,
    dest, failed, replica, from_one, from_two, from_four,
    base,
    dest_s, failed_s, dest_v, lost_counts, lost_sources,
    block_v, rows_v, extra_v, info_v, small_sem, block_sem, move_sem,
):
    lost_rows = fails * cap
    slots, width = base.shape[0], rows_v.shape[1]
    rows = block_v.shape[0] // fails
    half, eighth = width // 2, width // 8
    group = lax.axis_index("pipe")
    me = lax.axis_index("dp")
    small = [
        pltpu.make_async_copy(failed, failed_s, small_sem.at[0]),
        pltpu.make_async_copy(dest, dest_s, small_sem.at[1]),
        pltpu.make_async_copy(dest, dest_v, small_sem.at[2]),
    ]
    for copy in small:
        copy.start()
    for copy in small:
        copy.wait()
    blocks = [
        pltpu.make_async_copy(
            replica.at[pl.ds(pl.multiple_of(failed_s[i, group] * rows, rows), rows), :],
            block_v.at[pl.ds(i * rows, rows), :],
            block_sem.at[i],
        )
        for i in range(fails)
    ]
    for copy in blocks:
        copy.start()

    every = ranks * rows
    row_ids = lax.broadcasted_iota(jnp.int32, (every, every), 0)
    column_ids = lax.broadcasted_iota(jnp.int32, (every, every), 1)
    place = dest_v[pl.ds(group, 1), :]
    mine = jnp.where(lax.div(place, rows) == me, 1.0, 0.0)
    mine_down = jnp.sum(jnp.where(row_ids == column_ids, mine, 0.0), axis=1, keepdims=True)
    earlier = (row_ids < column_ids) & (lax.div(row_ids, rows) == lax.div(column_ids, rows))
    order = jnp.sum(jnp.where(earlier, mine_down, 0.0), axis=0, keepdims=True).astype(jnp.int32)
    columns = lax.broadcasted_iota(jnp.int32, (1, every), 1)
    slot_of = jnp.where(mine > 0.5, (lax.div(columns, rows) ^ me) * cap + order, -1)
    slot_rows = lax.broadcasted_iota(jnp.int32, (slots, every), 0)
    found = slot_rows == slot_of
    place_in = lax.rem(place, rows).astype(jnp.float32)
    places = jnp.sum(jnp.where(found, place_in + 1.0, 0.0), axis=1, keepdims=True) - 1.0
    slot_ids = lax.broadcasted_iota(jnp.int32, (slots, 128), 0)
    source = lax.div(slot_ids, cap) ^ me
    is_lost = source == failed_s[0, group]
    for i in range(1, fails):
        is_lost = is_lost | (source == failed_s[i, group])
    lanes = lax.broadcasted_iota(jnp.int32, (slots, 128), 1)
    info_v[...] = jnp.where(lanes == PLACE_LANE, places, jnp.where(is_lost, 1.0, 0.0))
    send_info = pltpu.make_async_copy(info_v, base.at[:, pl.ds(width, 128)], small_sem.at[0])
    send_info.start()
    for j in range(lost_rows):
        lost_sources[j] = 0
    for i in range(fails):
        lost_counts[i] = 0
        for r in range(rows):

            @pl.when(lax.div(dest_s[group, failed_s[i, group] * rows + r], rows) == me)
            def _(i=i, r=r):
                order = lost_counts[i]
                lost_sources[i * cap + order] = i * rows + r
                lost_counts[i] = order + 1

    is_failed = failed_s[0, group] == me
    sibling_failed = failed_s[0, group] == (me ^ 1)
    for i in range(1, fails):
        is_failed = is_failed | (failed_s[i, group] == me)
        sibling_failed = sibling_failed | (failed_s[i, group] == (me ^ 1))
    for copy in blocks:
        copy.wait()

    @pl.when(jnp.logical_not(is_failed))
    def _():
        rows_v[...] = block_v[...].astype(jnp.float32)

    @pl.when(is_failed)
    def _():
        def take(source, i, first, columns):
            return pltpu.make_async_copy(
                source.at[i, :, pl.ds(width, columns)], extra_v.at[pl.ds(i * cap, cap), pl.ds(first, columns)], move_sem
            )

        @pl.when(jnp.logical_not(sibling_failed))
        def _():
            copies = [take(from_one, i, 0, half) for i in range(fails)]
            for copy in copies:
                copy.start()
            for copy in copies:
                copy.wait()

        @pl.when(sibling_failed)
        def _():
            parts = (from_two.at[0], from_two.at[1], from_four.at[0], from_four.at[1])
            copies = [take(ref, i, n * eighth, eighth) for i in range(fails) for n, ref in enumerate(parts)]
            for copy in copies:
                copy.start()
            for copy in copies:
                copy.wait()

        packed = extra_v[...]
        rows_v[0:lost_rows, 0:half] = decode_short(signed_high(packed))
        rows_v[0:lost_rows, half:width] = decode_short(signed_low(packed))
        for j in range(lost_rows):
            lost_sources[j] = j

    moves = [
        pltpu.make_async_copy(
            rows_v.at[pl.ds(lost_sources[i * cap + order], 1), :],
            base.at[pl.ds((failed_s[i, group] ^ me) * cap + order, 1), pl.ds(0, width)],
            move_sem,
        )
        for i in range(fails)
        for order in range(cap)
    ]
    for copy in moves:
        copy.start()
    for copy in moves:
        copy.wait()
    send_info.wait()


def update_kernel(
    ranks, cap, elements,
    sums, base, *refs,
):
    kinds = sent_kinds(ranks)
    arrived = dict(zip(kinds, refs))
    for k, ref in zip(range(2, ranks, 2), refs[len(kinds):ranks]):
        arrived[k], arrived[k + 1] = arrived[k].at[0], ref.at[1]
    (new_master, new_first, new_second, info_s, sums_v, words, base_v,
     master_o, first_o, second_o, small_sem, word_sem, out_sem) = refs[ranks:]
    rows, width = new_master.shape
    slots = base_v.shape[0]
    info = pl.ds(width, 128)
    small = [
        pltpu.make_async_copy(source, target, small_sem.at[i])
        for i, (source, target) in enumerate(
            ((sums, sums_v), (base.at[:, info], base_v.at[:, info]), (base.at[:, info], info_s))
        )
    ]
    for copy in small:
        copy.start()
    for part, columns in enumerate(spans(width, UPDATE_PARTS)):
        copies = [pltpu.make_async_copy(base.at[:, columns], base_v.at[:, columns], word_sem.at[part])] + [
            pltpu.make_async_copy(
                arrived[k].at[:, :, columns], words.at[:, pl.ds(k * cap, cap), columns], word_sem.at[part]
            )
            for k in range(ranks)
        ]
        for copy in copies:
            copy.start()
    for copy in small:
        copy.wait()

    grad_total = jnp.sum(jnp.sum(sums_v[...], axis=0, keepdims=True), axis=1, keepdims=True)
    clip_scale = jnp.minimum(1.0, 1.0 / jnp.sqrt(grad_total / elements + clip_eps))
    is_lost = base_v[:, width + LOST_LANE:width + LOST_LANE + 1] > 0.5
    keep_one = jnp.where(is_lost, 0.0, beta_one)
    keep_two = jnp.where(is_lost, 0.0, beta_two)
    scale_one = 1.0 / (1.0 - beta_one**STEP)
    scale_two = 1.0 / (1.0 - beta_two**STEP)

    for part, columns in enumerate(spans(width, UPDATE_PARTS)):
        for ref in (words.at[:, :, columns], base_v.at[:, columns]):
            pltpu.make_async_copy(ref, ref, word_sem.at[part]).wait()
        one, two = words[0, :, columns], words[1, :, columns]
        weights = jnp.where(is_lost, base_v[:, columns], decode_log(signed_high(one), MASTER_MAX))
        first = decode_log(signed_low(one), FIRST_MAX)
        second = decode_second(lax.shift_right_logical(two, 16))
        grads = decode_short(signed_low(two)) * clip_scale
        first_new = keep_one * first + (1.0 - beta_one) * grads
        second_new = keep_two * second + (1.0 - beta_two) * grads * grads
        spread = second_new * scale_two
        root = spread * lax.rsqrt(jnp.maximum(spread, 1e-37))
        step = first_new * (learn_rate * scale_one) / (root + adam_eps)
        master_o[:, columns] = weights * (1.0 - learn_rate * decay_rate) - step
        first_o[:, columns] = first_new
        second_o[:, columns] = second_new
        for slot in range(slots):
            place = info_s[slot, PLACE_LANE].astype(jnp.int32)

            def move(slot=slot, place=place, columns=columns):
                return [
                    pltpu.make_async_copy(a.at[pl.ds(slot, 1), columns], b.at[pl.ds(place, 1), columns], out_sem)
                    for a, b in ((master_o, new_master), (first_o, new_first), (second_o, new_second))
                ]

            if slots == rows:
                for copy in move():
                    copy.start()
            else:

                @pl.when(place >= 0)
                def _(move=move):
                    for copy in move():
                        copy.start()

    for ref in (new_master, new_first, new_second):
        pltpu.make_async_copy(ref, ref, out_sem).wait()


def local(master, moment1, moment2, quant_grad, grad_exponent, replica_params, failed, dest):
    ranks = lax.axis_size("dp")
    devices = ranks * lax.axis_size("pipe")
    _, rows, width = master.shape
    failed = failed.T
    fails = failed.shape[0]
    assert fails == 2 and ranks >= 8 and ranks & (ranks - 1) == 0
    cap = (rows + ranks - 1) // ranks
    slots = ranks * cap
    kinds = sent_kinds(ranks)
    lost_rows = fails * cap
    i32, f32 = jnp.int32, jnp.float32
    vmem, smem, dma = pltpu.VMEM, pltpu.SMEM, pltpu.SemaphoreType.DMA

    packed = pl.pallas_call(
        functools.partial(pack_kernel, ranks, cap, fails, devices),
        out_shape=[jax.ShapeDtypeStruct(payload_shape(k, cap, width), i32) for k in kinds]
        + [pltpu.VMEM((devices, 128), f32)],
        in_specs=[ANY] * 8,
        out_specs=[ANY] * (len(kinds) + 1),
        scratch_shapes=[
            smem(dest.shape, i32), smem(failed.shape, i32), smem((1, rows), i32),
            smem((ranks,), i32), smem((slots,), i32),
            smem((ranks * fails,), i32), smem((ranks * lost_rows,), i32),
            vmem((rows, width), f32), vmem((rows, width), f32), vmem((rows, width), f32),
            vmem((rows, width), jnp.bfloat16),
            vmem((fails * rows, width), jnp.bfloat16), vmem((fails * rows, width), f32),
            vmem((lost_rows, width), f32),
            vmem((2, rows, width), i32),
            vmem((lost_rows, width // 2), i32), vmem((devices, 128), f32),
            dma((3,)), dma((len(PACK_PARTS), 4)), dma((fails,)), dma, dma,
        ],
        compiler_params=pltpu.CompilerParams(vmem_limit_bytes=PACK_VMEM),
        name="pack",
    )(dest, failed, grad_exponent, master[0], moment1[0], moment2[0], quant_grad[0], replica_params[0, 0])
    payloads, total = dict(zip(kinds, packed)), packed[-1]

    def send(k, value):
        return lax.ppermute(value, "dp", [(i, i ^ k) for i in range(ranks)])

    arrived = {0: payloads[0], 1: send(1, payloads[1])}
    for k in range(2, ranks, 2):
        value = payloads[k]
        if k not in (2, 4):
            value, _ = lax.optimization_barrier((value, arrived[1]))
        arrived[k] = send(k, value)
    sums = lax.all_to_all(total, ("pipe", "dp"), split_axis=0, concat_axis=0, tiled=True)
    handed = []
    for k in range(2, ranks, 2):
        value, _ = lax.optimization_barrier((arrived[k], sums))
        handed.append(send(1, value))

    base = pl.pallas_call(
        functools.partial(base_kernel, ranks, cap, fails),
        out_shape=jax.ShapeDtypeStruct((slots, width + 128), f32),
        in_specs=[ANY] * 6,
        out_specs=ANY,
        scratch_shapes=[
            smem(dest.shape, i32), smem(failed.shape, i32), vmem(dest.shape, i32),
            smem((fails,), i32), smem((lost_rows,), i32),
            vmem((fails * rows, width), jnp.bfloat16), vmem((fails * rows, width), f32),
            vmem((lost_rows, width // 2), i32), vmem((slots, 128), f32),
            dma((3,)), dma((fails,)), dma,
        ],
        compiler_params=pltpu.CompilerParams(vmem_limit_bytes=OTHER_VMEM),
        name="base",
    )(dest, failed, replica_params[0, 0], arrived[1], arrived[2], arrived[4])

    outs = pl.pallas_call(
        functools.partial(update_kernel, ranks, cap, devices * rows * width),
        out_shape=[jax.ShapeDtypeStruct((rows, width), f32)] * 3,
        in_specs=[ANY] * (2 + ranks),
        out_specs=[ANY] * 3,
        scratch_shapes=[
            smem((slots, 128), f32), vmem((devices, 128), f32),
            vmem((2, slots, width), i32), vmem((slots, width + 128), f32),
            vmem((slots, width), f32), vmem((slots, width), f32), vmem((slots, width), f32),
            dma((3,)), dma((len(UPDATE_PARTS),)), dma,
        ],
        compiler_params=pltpu.CompilerParams(vmem_limit_bytes=OTHER_VMEM),
        name="update",
    )(sums, base, *[arrived[k] for k in kinds], *handed)
    return tuple(out[None] for out in outs)


def solution(mesh):
    rows3 = P("pipe", "dp", None)
    in_specs = (rows3, rows3, rows3, rows3, P("pipe", "dp"), P("pipe", "dp", None, None), P(), P())
    return jax.shard_map(local, mesh=mesh, in_specs=in_specs, out_specs=(rows3,) * 3, check_vma=False)
```
